32 devices in a mesh: parts: 2 (over y), wide: 16 (over z, x, core).
Axes of the slice: x: 2, y: 2, z: 4, core: 2. Of those that a mesh axis runs over, the one named last changes fastest.
Arguments:
- amplitudes: bfloat16 [2048, 262144], P(('parts', 'wide')), parts along dimension 0, may hold values from -6 to 6
- integrals: bfloat16 [2048, 262144], P('parts', 'wide'), parts along dimension 0, may hold values from -0.03125 to 0.03125
- occ_irrep: int32 [64], P('parts'), parts along dimension 0, may hold values from 0 to 7
- vir_irrep: int32 [16], P('parts'), parts along dimension 0, may hold values from 0 to 7, as said below
- occ_energy: float32 [64], P('parts'), parts along dimension 0, may hold values from -1.5 to -0.5
- vir_energy: float32 [1024], P('parts'), parts along dimension 0, may hold values from 0.5 to 2.5
Outputs:
- ladder: float32 [2048, 1024], P(('parts', 'wide')), parts along dimension 0
The draws below stay inside these ranges and needn't reach their ends.
There are 2 independent parts, one for each index of `parts`. The reference program is written for one: setup_inputs(seed, part) draws one part's arguments, and reference() takes and returns one part's arrays. A program takes and returns all parts, laid end to end along the dimension named above; each array names one. Nothing has to cross between parts.
Inputs may be any that keep to these rules, and one draw needn't show every extreme that they name: `vir_irrep`: 6 of the blocks carry one common label, which lies between 1 and 6; of the other two blocks one carries label 0 and one label 7. Which blocks these are is arbitrary.
All inputs are finite; a program needn't handle non-finite values.
Results may differ from the reference program's by a relative error of at most 0.0003.
Values may be sent and summed in bfloat16 or wider, within the bound.
No kernel may reach another device: no remote copies, remote signals or barrier semaphores. Data moves between devices by JAX's collectives and lax.ppermute only.
A program may use at most 256 MiB of HBM per device.

```python
import jax
import jax.numpy as jnp
from jax import lax

NO = 32
NV = 512
BLK = 64
SLAB_A = 2
NB = 8
PAIRS = 1024
VPAIRS = 262144
SLAB = 1024


def draw_vir_irrep(key, part):
    key = jax.random.fold_in(key, 11)
    key_label, key_order = jax.random.split(key)
    common = jax.random.randint(key_label, (), 1, 7, dtype=jnp.int32)
    order = jax.random.permutation(key_order, NB).astype(jnp.int32)
    labels = jnp.where(order == 0, 0, jnp.where(order == 1, 7, common))
    return labels.astype(jnp.int32)


def plant(drawn, key, smallest, largest):
    longest = drawn.shape.index(max(drawn.shape))
    spots = []
    for shift in (0, 1):
        where = [jax.random.randint(jax.random.fold_in(key, axis), (), 0, length) for axis, length in enumerate(drawn.shape)]
        where[longest] = (where[longest] + shift) % drawn.shape[longest]
        spots.append(tuple(where))
    return drawn.at[spots[0]].set(smallest).at[spots[1]].set(largest)


def block_levels(key, dims, pieces, smallest, high):
    level = 1.0
    for dim, parts in pieces:
        draws = jax.random.uniform(jax.random.fold_in(jax.random.fold_in(key, 6), dim), (parts,), jnp.float32, smallest / len(pieces), high / len(pieces))
        level = level * jnp.repeat(jnp.exp(draws), dims[dim] // parts).reshape((-1,) + (1,) * (len(dims) - 1 - dim))
    return level


def bell_draw(rng, shape, deviation, most, shards=(), kind=jnp.bfloat16):
    level = block_levels(rng, shape, shards, -0.22, 0.18) if shards else 1.0
    array = jax.random.normal(rng, shape, jnp.float32) * deviation * level
    return jnp.minimum(jnp.maximum(array, -most), most).astype(kind)


def setup_inputs(seed: int = 0, part: int = 0) -> dict:
    key_of = jax.random.split(jax.random.key(seed), 7)
    part_splits = jax.random.split(jax.random.fold_in(key_of[6], part), 7)
    amplitudes = bell_draw(part_splits[0], (PAIRS, VPAIRS), 1.0, 6.0, ((0, 16),))
    integrals = bell_draw(part_splits[1], (SLAB, VPAIRS), (NV * NV // 8) ** -0.5, 0.03125, ((1, 16),))
    occ_irrep = plant(jax.random.randint(part_splits[2], (NO,), 0, 8), jax.random.fold_in(part_splits[2], 1), 0, 7).astype(jnp.int32)
    vir_irrep = draw_vir_irrep(jax.random.fold_in(jax.random.fold_in(key_of[6], part), 71), part)
    occ_energy = jnp.clip(jax.random.uniform(part_splits[4], (NO,), jnp.float32, -1.5, -0.5), -1.5, -0.5)
    vir_energy = jnp.clip(jax.random.uniform(part_splits[5], (NV,), jnp.float32, 0.5, 2.5), 0.5, 2.5)
    return {"amplitudes": amplitudes, "integrals": integrals, "occ_irrep": occ_irrep, "vir_irrep": vir_irrep, "occ_energy": occ_energy, "vir_energy": vir_energy}


def block_lookup(table, block_ids):
    labels = jnp.arange(table.shape[0], dtype=jnp.int32)
    hits = block_ids[:, None] == labels[None, :]
    return jnp.sum(jnp.where(hits, table[None, :], 0), axis=1).astype(jnp.int32)


def reference(amplitudes, integrals, occ_irrep, vir_irrep, occ_energy, vir_energy):
    vir_ids = jnp.arange(NV, dtype=jnp.int32)
    vir_label = block_lookup(vir_irrep, vir_ids // BLK)
    pair_irrep = jnp.bitwise_xor(occ_irrep[:, None], occ_irrep[None, :]).reshape(-1)
    slab_irrep = jnp.bitwise_xor(vir_label[:SLAB_A, None], vir_label[None, :]).reshape(-1)
    block_width = BLK * NV

    def add_block(block_id, total):
        col_start = (block_id * block_width).astype(jnp.int32)
        tau_block = lax.dynamic_slice_in_dim(amplitudes, col_start, block_width, 1)
        int_block = lax.dynamic_slice_in_dim(integrals, col_start, block_width, 1)
        first_label = lax.dynamic_slice_in_dim(vir_label, (block_id * BLK).astype(jnp.int32), BLK, 0)
        col_irrep = jnp.bitwise_xor(first_label[:, None], vir_label[None, :]).reshape(-1)
        kept_t = jnp.where(pair_irrep[:, None] == col_irrep[None, :], tau_block, 0).astype(jnp.bfloat16)
        kept_v = jnp.where(slab_irrep[:, None] == col_irrep[None, :], int_block, 0).astype(jnp.bfloat16)
        return total + jnp.dot(kept_t.astype(jnp.float32), kept_v.astype(jnp.float32).T, preferred_element_type=jnp.float32)

    total = lax.fori_loop(0, NB, add_block, jnp.zeros((NO * NO, SLAB_A * NV), jnp.float32))
    slab_energy = (vir_energy[:SLAB_A, None] + vir_energy[None, :]).reshape(-1)
    pair_energy = (occ_energy[:, None] + occ_energy[None, :]).reshape(-1)
    denominator = slab_energy[None, :] - pair_energy[:, None]
    return total / denominator
```

```python
import jax
import jax.numpy as jnp
from jax import lax
from jax.experimental import pallas as pl
from jax.experimental.pallas import tpu as pltpu
from jax.sharding import PartitionSpec as P

BLK = 64
LANE = 128
SUB = 8
NBLK = 8
CORES = 2
ROWCAP = 256
CHUNKS = ((0, 4), (16, 16), (8, 8), (4, 4))
LEVELS = ((96, 24), (128, 24))
MOST = max(cap for cap, _ in LEVELS)
CHIP, CORE, PURE, TILE_A, TILE_B, ROLL, TILE_U, TILE_W, HALF, KIND, ROLE, LEVEL = 0, 1, 2, 4, 5, 6, 7, 8, 9, 16, 24, 27
START, COUNT, ROW_CLASS, ROW_RANK, SIZE = 32, 96, 128, 192, 256
TYPES = ((0, 1, 2), (1, 0, 3), (2, 3, 0))
SMEM = pltpu.SMEM
VMEM = pltpu.VMEM
GRANT = 48 * 1024 * 1024
BF = jnp.bfloat16
F32 = jnp.float32
I32 = jnp.int32


def block_lookup(table, block_ids):
    labels = jnp.arange(table.shape[0], dtype=jnp.int32)
    hits = block_ids[:, None] == labels[None, :]
    return jnp.sum(jnp.where(hits, table[None, :], 0), axis=1)


def contract(left, right):
    return lax.dot_general(
        left, right, (((1,), (1,)), ((), ())), preferred_element_type=jnp.float32
    )


def dense_body(amplitudes, integrals, occ_irrep, vir_irrep, occ_energy, vir_energy):
    position = lax.axis_index("wide")
    pairs_local = amplitudes.shape[0]
    local_cols = integrals.shape[1]
    nvir = vir_energy.shape[0]
    slab_rows = integrals.shape[0]
    slab_first = slab_rows // nvir
    gathered = lax.all_to_all(amplitudes, "wide", split_axis=1, concat_axis=0, tiled=True)
    flat_cols = position * local_cols + jnp.arange(local_cols, dtype=jnp.int32)
    first_vir = flat_cols // nvir
    second_vir = flat_cols % nvir
    col_irrep = jnp.bitwise_xor(
        block_lookup(vir_irrep, first_vir // BLK), block_lookup(vir_irrep, second_vir // BLK)
    )
    vir_label = block_lookup(vir_irrep, jnp.arange(nvir, dtype=jnp.int32) // BLK)
    pair_irrep = jnp.bitwise_xor(occ_irrep[:, None], occ_irrep[None, :]).reshape(-1)
    slab_irrep = jnp.bitwise_xor(vir_label[:slab_first, None], vir_label[None, :]).reshape(-1)
    kept_t = jnp.where(pair_irrep[:, None] == col_irrep[None, :], gathered, 0)
    kept_v = jnp.where(slab_irrep[:, None] == col_irrep[None, :], integrals, 0)
    summed = lax.psum_scatter(contract(kept_t, kept_v), "wide", scatter_dimension=0, tiled=True)
    slab_energy = (vir_energy[:slab_first, None] + vir_energy[None, :]).reshape(-1)
    pair_energy = (occ_energy[:, None] + occ_energy[None, :]).reshape(-1)
    local_pair_energy = lax.dynamic_slice_in_dim(
        pair_energy, position * pairs_local, pairs_local, 0
    )
    denominator = slab_energy[None, :] - local_pair_energy[:, None]
    return summed / denominator


def tile(ref, lead, c, which):
    start = pl.multiple_of(c * NBLK * BLK + which * LANE, LANE)
    return ref[lead + (slice(None), pl.ds(start, LANE))]


def maybe_roll(x, flag):
    return jnp.where(flag == 1, jnp.concatenate([x[:, BLK:], x[:, :BLK]], axis=1), x)


def half_masks(table, shape):
    half = (lax.broadcasted_iota(I32, shape, 1) % LANE) // BLK
    first = half == table[HALF]
    return jnp.where(first, 1.0, 0.0).astype(BF), jnp.where(first, 0.0, 1.0).astype(BF)


def setup_kernel(
    devices, nslab, place, occ, vir, occ_here, occ_lane, occ_rows, table, pick_ref, big_ref, a_ref, b_ref, class_ref, hist, tally
):
    chips = devices // CORES
    nocc = occ.shape[0]
    per_device = nocc // devices
    chip, core = place[0], place[1]
    table[CHIP] = chip
    table[CORE] = core
    common, zero_at, seven_at = vir[0] * 0, vir[0] * 0, vir[0] * 0
    for b in range(NBLK):
        label = vir[b]
        common = jnp.where((label != 0) & (label != 7), label, common)
        zero_at = jnp.where(label == 0, b, zero_at)
        seven_at = jnp.where(label == 7, b, seven_at)
        table[KIND + b] = jnp.where(label == 0, 1, jnp.where(label == 7, 2, 0))
    irreps = [common * 0, common, common ^ 7, common * 0 + 7]
    needed = []
    for g in range(4):
        some = common * 0
        for b in range(NBLK):
            some = jnp.where((vir[0] ^ vir[b]) == irreps[g], 1, some)
        needed.append(some)

    tile_a, half_a = zero_at // 2, zero_at % 2
    same = seven_at // 2 == tile_a
    tile_b = jnp.where(same, (tile_a + 1) % 4, seven_at // 2)
    pure = jnp.where((tile_a != 0) & (tile_b != 0), 0, jnp.where((tile_a != 1) & (tile_b != 1), 1, 2))
    table[PURE] = pure
    table[PURE + 1] = 6 - tile_a - tile_b - pure
    table[TILE_A] = tile_a
    table[TILE_B] = tile_b
    table[ROLL] = jnp.where(same | (seven_at % 2 != half_a), 0, 1)
    table[TILE_U] = jnp.where(same, tile_a, tile_b)
    table[TILE_W] = jnp.where(same, tile_b, tile_a)
    table[HALF] = half_a

    for h in range(NBLK):
        hist[h] = 0
    for j in range(nocc):
        hist[NBLK + j] = hist[occ[j]]
        hist[occ[j]] = hist[occ[j]] + 1
    of_i = lambda i, g: hist[occ[i] ^ irreps[g]] * needed[g]
    biggest = common * 0
    most_class = common * 0
    for g in range(4):
        total = common * 0
        for s in range(devices):
            table[START + g * devices + s] = total
            here = common * 0
            for i in range(per_device):
                here += of_i(s * per_device + i, g)
            total += here
            biggest = jnp.maximum(biggest, here)
            tally[g * devices + s] = here
        most_class = jnp.maximum(most_class, total)
        for c in range(chips):
            table[COUNT + g * chips + c] = tally[g * devices + c * CORES] + tally[g * devices + c * CORES + 1]
    most = common * 0
    for c in range(chips):
        n = [table[COUNT + g * chips + c] for g in range(4)]
        for b, a, s in TYPES:
            most = jnp.maximum(most, 3 * n[b] + jnp.maximum(n[a], n[s]))
    level = common * 0 + len(LEVELS)
    for at in range(len(LEVELS) - 1, -1, -1):
        cap, cap_back = LEVELS[at]
        level = jnp.where((most <= cap) & (biggest <= cap_back) & (most_class <= ROWCAP), at, level)
    table[LEVEL] = level

    my_kind = table[KIND + chip]
    roles = [jnp.where(my_kind == 0, x, jnp.where(my_kind == 1, y, z)) for x, y, z in zip(*TYPES)]
    for n in range(3):
        table[ROLE + n] = roles[n]
    position = chip * CORES + core
    for i in range(per_device):
        at = position * per_device + i
        for j in range(nocc):
            both = occ[at] ^ occ[j]
            kind = common * 0 + 4
            rank = hist[NBLK + j]
            for g in range(4):
                hit = (both == irreps[g]) & (needed[g] == 1)
                kind = jnp.where(hit, g, kind)
                for before in range(i):
                    rank = rank + jnp.where(hit, of_i(position * per_device + before, g), 0)
            table[ROW_CLASS + i * nocc + j] = kind
            table[ROW_RANK + i * nocc + j] = rank

    width = CORES * per_device * nocc
    lane = lax.broadcasted_iota(I32, (1, width), 1)
    earlier = lax.broadcasted_iota(I32, (nocc, width), 0) < lax.broadcasted_iota(I32, (nocc, width), 1) % nocc
    alike = jnp.where((occ_rows[...] == occ_lane[...]) & earlier, 1, 0)
    rank = jnp.sum(alike, axis=0, keepdims=True)
    irrep = occ_lane[...] ^ occ_here[...]
    spots = []
    for g in range(4):
        base, run = jnp.zeros((1, width), I32), common * 0
        for i in range(CORES * per_device):
            shown = i ^ (core * per_device)
            base = jnp.where(lane // nocc == shown, run, base)
            run += of_i(chip * CORES * per_device + i, g)
        spots.append((jnp.where((irrep == irreps[g]) & (needed[g] == 1), base + rank, -4 * MOST), run))
    slot = lax.broadcasted_iota(I32, (MOST, width), 0)
    for t, (b, a, s) in enumerate(TYPES):
        for section, (g, f) in enumerate(((b, 0), (b, 1), (b, 2), (a, 3), (s, 3))):
            target = spots[g][0] + f * spots[b][1]
            pick_ref[t, :, section * width : (section + 1) * width] = jnp.where(slot == target, 1.0, 0.0).astype(BF)

    half = lax.broadcasted_iota(I32, (BLK, LANE), 1) // BLK == half_a
    column = lax.broadcasted_iota(I32, class_ref.shape, 1) % (NBLK * BLK) // BLK
    column_class = jnp.zeros(class_ref.shape, I32)
    for b in range(NBLK):
        both = vir[0] ^ vir[b]
        kind = common * 0 + 4
        for g in range(4):
            kind = jnp.where(both == irreps[g], g, kind)
        column_class = jnp.where(column == b, kind, column_class)
        is_ = [jnp.where(kind == roles[n], 1.0, 0.0) for n in range(3)]
        full = jnp.zeros((BLK, LANE), F32)
        for a in range(nslab):
            rows = slice((a * NBLK + b) * BLK, (a * NBLK + b + 1) * BLK)
            big_ref[rows, :] = (full + is_[0]).astype(BF)
            a_ref[rows, :] = jnp.where(half, full + is_[1], 0.0).astype(BF)
            b_ref[rows, :] = jnp.where(half, 0.0, full + is_[2]).astype(BF)
    class_ref[...] = column_class


def setup(place, occ, vir, slab_rows, devices):
    nocc = occ.shape[0]
    width = CORES * nocc // devices * nocc
    per_chip = width // nocc
    chip, core = place[0], place[1]
    mine = lax.dynamic_slice_in_dim(occ, chip * per_chip, per_chip, 0).reshape(CORES, -1)
    mine = jnp.where(core == 0, mine, mine[::-1]).reshape(-1)
    occ_here = jnp.repeat(mine, nocc)[None, :]
    occ_lane = jnp.tile(occ, per_chip)[None, :]
    occ_rows = jnp.broadcast_to(occ[:, None], (nocc, width))
    smem, vmem = pl.BlockSpec(memory_space=SMEM), pl.BlockSpec(memory_space=VMEM)
    mask = jax.ShapeDtypeStruct((slab_rows, LANE), BF)
    return pl.pallas_call(
        lambda *refs: setup_kernel(devices, slab_rows // (NBLK * BLK), *refs),
        in_specs=[smem] * 3 + [vmem] * 3,
        out_specs=[smem] + [vmem] * 5,
        out_shape=[
            jax.ShapeDtypeStruct((SIZE,), I32),
            jax.ShapeDtypeStruct((3, MOST, 5 * width), BF),
            mask,
            mask,
            mask,
            jax.ShapeDtypeStruct((1, slab_rows), I32),
        ],
        scratch_shapes=[SMEM((NBLK + nocc,), I32), SMEM((4 * devices,), I32)],
        name="setup",
    )(place, occ, vir, occ_here, occ_lane, occ_rows)


def take_kernel(chips, table, *refs):
    for d in range(chips):
        refs[chips][d] = refs[d][...]


def take_for_sibling(table, amplitudes, first, count, cols_device):
    rows, width = amplitudes.shape[0], count * NBLK * BLK
    chips = amplitudes.shape[1] // cols_device // CORES
    step = 2 * NBLK * BLK
    per_device = cols_device // step

    def column(d):
        return lambda q, s: (0, ((s[CHIP] ^ d) * CORES + 1 - s[CORE]) * per_device + first // 2 + q)

    return pl.pallas_call(
        lambda *refs: take_kernel(chips, *refs),
        grid_spec=pltpu.PrefetchScalarGridSpec(
            num_scalar_prefetch=1,
            grid=(width // step,),
            in_specs=[pl.BlockSpec((rows, step), column(d)) for d in range(chips)],
            out_specs=pl.BlockSpec((chips, rows, step), lambda q, s: (0, 0, q)),
        ),
        out_shape=jax.ShapeDtypeStruct((chips, rows, width), amplitudes.dtype),
        cost_estimate=pl.CostEstimate(flops=0, bytes_accessed=4 * chips * rows * width, transcendentals=0),
        name="take_for_sibling",
    )(table, *[amplitudes] * chips)


def pack_kernel(count, chips, table, own_ref, sib_ref, pick_ref, *rest):
    outs, held = rest[:chips], rest[chips]
    d = pl.program_id(0)
    pick = pick_ref[0]
    mine, other = half_masks(table, (own_ref.shape[0], LANE))
    for u in range(count // 2):
        columns = []
        for c in (2 * u, 2 * u + 1):
            parts = [[], [], [], [], []]
            for ref, lead in ((own_ref, ()), (sib_ref, (0,))):
                at = lambda n: tile(ref, lead, c, table[n])
                parts[0].append(at(PURE))
                parts[1].append(at(PURE + 1))
                parts[2].append(at(TILE_W) * other + maybe_roll(at(TILE_B), table[ROLL]) * mine)
                parts[3].append(at(TILE_A) * mine)
                parts[4].append(maybe_roll(at(TILE_U), table[ROLL]) * other)
            columns.append(jnp.concatenate([x for part in parts for x in part], axis=0))
        rows = jnp.concatenate(columns, axis=1)
        held[:, u * 2 * LANE : (u + 1) * 2 * LANE] = jnp.dot(pick, rows, preferred_element_type=F32).astype(BF)
    for i in range(chips):

        @pl.when(d == i)
        def _():
            outs[i][...] = held[...]


def pack(table, amplitudes, sibling, pick, cap, first, count, cols_device):
    rows, width = amplitudes.shape[0], count * NBLK * BLK
    chips = amplitudes.shape[1] // cols_device // CORES
    per_device = cols_device // width

    def column(d, s):
        return (0, ((s[CHIP] ^ d) * CORES + s[CORE]) * per_device + first // count)

    out = jax.ShapeDtypeStruct((cap, count * LANE), BF)
    return pl.pallas_call(
        lambda *refs: pack_kernel(count, chips, *refs),
        grid_spec=pltpu.PrefetchScalarGridSpec(
            num_scalar_prefetch=1,
            grid=(chips,),
            in_specs=[
                pl.BlockSpec((rows, width), column),
                pl.BlockSpec((1, rows, width), lambda d, s: (d, 0, 0)),
                pl.BlockSpec((1, cap, pick.shape[2]), lambda d, s: (s[KIND + (s[CHIP] ^ d)], 0, 0)),
            ],
            out_specs=[pl.BlockSpec(out.shape, lambda d, s: (0, 0))] * chips,
            scratch_shapes=[pltpu.VMEM(out.shape, BF)],
        ),
        out_shape=[out] * chips,
        compiler_params=pltpu.CompilerParams(vmem_limit_bytes=GRANT),
        cost_estimate=pl.CostEstimate(
            flops=2 * chips * count * LANE * cap * 10 * rows,
            bytes_accessed=4 * chips * rows * width + 2 * chips * cap * count * LANE,
            transcendentals=0,
        ),
        name="pack",
    )(table, amplitudes, sibling, pick)


def spread_kernel(chips, cap, table, spread_ref):
    column = lax.broadcasted_iota(I32, (1, chips * cap), 1)
    row = lax.broadcasted_iota(I32, (ROWCAP, chips * cap), 0)
    for section, (n, f) in enumerate(((0, 0), (0, 1), (0, 2), (1, 3), (2, 3))):
        target = jnp.full((1, chips * cap), -1, I32)
        for d in range(chips):
            chip = table[CHIP] ^ d
            group = table[ROLE + n]
            k = column - d * cap - f * table[COUNT + table[ROLE] * chips + chip]
            count = table[COUNT + group * chips + chip]
            start = table[START + (group * chips + chip) * CORES]
            inside = (column >= d * cap) & (column < (d + 1) * cap) & (k >= 0) & (k < count)
            target = jnp.where(inside, start + k, target)
        spread_ref[section * ROWCAP : (section + 1) * ROWCAP, :] = jnp.where(row == target, 1.0, 0.0).astype(BF)


def make_spread(table, chips, cap):
    return pl.pallas_call(
        lambda *refs: spread_kernel(chips, cap, *refs),
        in_specs=[pl.BlockSpec(memory_space=SMEM)],
        out_specs=pl.BlockSpec(memory_space=VMEM),
        out_shape=jax.ShapeDtypeStruct((5 * ROWCAP, chips * cap), BF),
        compiler_params=pltpu.CompilerParams(vmem_limit_bytes=GRANT),
        cost_estimate=pl.CostEstimate(flops=0, bytes_accessed=10 * ROWCAP * chips * cap, transcendentals=0),
        name="make_spread",
    )(table)


def contract_kernel(chips, table, *refs):
    parts, (vals, spread_ref, big_ref, a_ref, b_ref, acc_ref, out_ref) = refs[:chips], refs[chips:]

    @pl.when(pl.program_id(0) == 0)
    def _():
        out_ref[...] = acc_ref[...]

    received = jnp.concatenate([r[...] for r in parts], axis=0)
    spread = jnp.dot(spread_ref[...], received, preferred_element_type=F32)
    left = [spread[j * ROWCAP : (j + 1) * ROWCAP] for j in range(5)]
    half = (lax.broadcasted_iota(I32, (ROWCAP, 2 * LANE), 1) % LANE) // BLK
    left = [x.astype(BF) for x in left[:3] + [jnp.where(half == table[HALF], left[3], left[4])]]
    mine, other = half_masks(table, (vals.shape[0], LANE))
    right = [[], [], [], []]
    for c in (0, 1):
        at = lambda n: tile(vals, (), c, table[n])
        right[0].append(at(PURE) * big_ref[...])
        right[1].append(at(PURE + 1) * big_ref[...])
        right[2].append((at(TILE_W) * other + maybe_roll(at(TILE_B), table[ROLL]) * mine) * big_ref[...])
        right[3].append(at(TILE_A) * a_ref[...] + maybe_roll(at(TILE_U), table[ROLL]) * b_ref[...])
    total = out_ref[...]
    for j in range(4):
        total += contract(jnp.concatenate(right[j], axis=1), left[j])
    out_ref[...] = total


def contract_chunk(table, received, integrals, spread, masks, acc, first, count):
    chips = len(received)
    cap = received[0].shape[0]
    slab = integrals.shape[0]
    fixed = lambda u, s: (0, 0)
    return pl.pallas_call(
        lambda *refs: contract_kernel(chips, *refs),
        grid_spec=pltpu.PrefetchScalarGridSpec(
            num_scalar_prefetch=1,
            grid=(count // 2,),
            in_specs=[pl.BlockSpec((cap, 2 * LANE), lambda u, s: (0, u))] * chips
            + [pl.BlockSpec((slab, 2 * NBLK * BLK), lambda u, s: (0, first // 2 + u))]
            + [pl.BlockSpec(x.shape, fixed) for x in (spread, *masks, acc)],
            out_specs=pl.BlockSpec(acc.shape, fixed),
        ),
        out_shape=jax.ShapeDtypeStruct(acc.shape, F32),
        compiler_params=pltpu.CompilerParams(vmem_limit_bytes=GRANT),
        cost_estimate=pl.CostEstimate(
            flops=2 * count * LANE * (5 * ROWCAP * chips * cap + 4 * ROWCAP * slab),
            bytes_accessed=2 * slab * count * NBLK * BLK + 8 * acc.shape[0] * slab,
            transcendentals=0,
        ),
        name="contract_chunk",
    )(table, *received, integrals, spread, *masks, acc)


def split_kernel(chips, cap, table, sums_ref, class_ref, own_ref, sib_ref, held):
    d = pl.program_id(0)

    @pl.when(d == 0)
    def _():
        held[:ROWCAP, :] = sums_ref[...].T
        held[ROWCAP:, :] = jnp.zeros((cap + SUB, held.shape[1]), F32)

    for flip, ref in ((0, own_ref), (1, sib_ref)):
        device = (table[CHIP] ^ d) * CORES + (table[CORE] ^ flip)
        rows = []
        for g in range(4):
            start = table[START + g * chips * CORES + device]
            odd = start % SUB
            window = held[pl.ds(pl.multiple_of(start - odd, SUB), cap + SUB), :]
            rows.append(pltpu.roll(window, (cap + SUB - odd) % (cap + SUB), 0)[:cap])
        kind = class_ref[...]
        ref[0] = jnp.where(kind == 0, rows[0], jnp.where(kind == 1, rows[1], jnp.where(kind == 2, rows[2], rows[3])))


def split(table, sums, column_class, chips, cap):
    slab = sums.shape[0]
    out = jax.ShapeDtypeStruct((chips, cap, slab), F32)
    fixed = lambda d, s: (0, 0)
    return pl.pallas_call(
        lambda *refs: split_kernel(chips, cap, *refs),
        grid_spec=pltpu.PrefetchScalarGridSpec(
            num_scalar_prefetch=1,
            grid=(chips,),
            in_specs=[pl.BlockSpec(sums.shape, fixed), pl.BlockSpec((1, slab), fixed)],
            out_specs=[pl.BlockSpec((1, cap, slab), lambda d, s: (d, 0, 0))] * 2,
            scratch_shapes=[pltpu.VMEM((ROWCAP + cap + SUB, slab), F32)],
        ),
        out_shape=[out, out],
        cost_estimate=pl.CostEstimate(flops=0, bytes_accessed=4 * sums.size + 8 * out.size, transcendentals=0),
        name="split_sums",
    )(table, sums, column_class)


def add_kernel(own_ref, sib_ref, *outs):
    for d, ref in enumerate(outs):
        ref[...] = own_ref[d] + sib_ref[d]


def add_cores(own, sibling):
    out = jax.ShapeDtypeStruct(own.shape[1:], F32)
    return pl.pallas_call(
        add_kernel,
        out_shape=[out] * own.shape[0],
        cost_estimate=pl.CostEstimate(flops=own.size, bytes_accessed=12 * own.size, transcendentals=0),
        name="add_cores",
    )(own, sibling)


def finish_kernel(count, pairs, table, energies, class_ref, slab_ref, *refs):
    parts, out_ref, held = refs[:count], refs[count], refs[count + 1]
    total = parts[0][...]
    for ref in parts[1:]:
        total = total + ref[...]
    held[...] = total
    for p in range(pairs):
        kind = table[ROW_CLASS + p]
        row = held[pl.ds(jnp.where(kind < 4, table[ROW_RANK + p], 0), 1), :]
        kept = jnp.where(class_ref[...] == kind, row, 0.0)
        out_ref[p : p + 1, :] = kept / (slab_ref[...] - energies[p])


def finish(table, parts, energies, column_class, slab_energy):
    pairs, slab = energies.shape[0], column_class.shape[1]
    smem, vmem = pl.BlockSpec(memory_space=SMEM), pl.BlockSpec(memory_space=VMEM)
    return pl.pallas_call(
        lambda *refs: finish_kernel(len(parts), pairs, *refs),
        in_specs=[smem] * 2 + [vmem] * (2 + len(parts)),
        out_specs=vmem,
        out_shape=jax.ShapeDtypeStruct((pairs, slab), F32),
        scratch_shapes=[pltpu.VMEM(parts[0].shape, F32)],
        cost_estimate=pl.CostEstimate(flops=4 * pairs * slab, bytes_accessed=8 * pairs * slab, transcendentals=0),
        name="finish",
    )(table, energies, column_class, slab_energy, *parts)


def body(amplitudes, integrals, occ_irrep, vir_irrep, occ_energy, vir_energy):
    devices = lax.axis_size("wide")
    pairs_local = amplitudes.shape[0]
    cols = integrals.shape[1]
    slab_rows = integrals.shape[0]
    nvir = vir_energy.shape[0]
    nocc = occ_irrep.shape[0]
    given = (amplitudes, integrals, occ_irrep, vir_irrep, occ_energy, vir_energy)
    compact = (
        nvir == NBLK * BLK
        and CORES * cols == BLK * nvir
        and cols == sum(count for _, count in CHUNKS) * nvir
        and pairs_local % 16 == 0
        and devices == 16
        and nocc == 32
        and devices * pairs_local == nocc * nocc
        and lax.axis_size("parts") == 2
    )
    if not compact:
        return dense_body(*given)

    chips = devices // CORES
    position = lax.axis_index("wide")
    place = jnp.stack([position // CORES, position % CORES]).astype(I32)
    swap = [(i, i ^ 1) for i in range(devices)]
    routes = [[(i, i ^ (d * CORES)) for i in range(devices)] for d in range(chips)]
    table, pick, big, mask_a, mask_b, column_class = setup(place, occ_irrep, vir_irrep, slab_rows, devices)
    level = table[LEVEL : LEVEL + 1]
    level = jnp.maximum(level, lax.ppermute(level, "parts", [(0, 1), (1, 0)]))[0]

    def from_sibling(first, count):
        return lax.ppermute(take_for_sibling(place, amplitudes, first, count, cols), "wide", swap)

    early = from_sibling(*CHUNKS[0])

    def compact_plan(cap, cap_back):
        def run(amplitudes, integrals, early):
            spread = make_spread(table, chips, cap)
            sent = []
            for n, (first, count) in enumerate(CHUNKS):
                sibling = early if n == 0 else from_sibling(first, count)
                packed = pack(table, amplitudes, sibling, pick, cap, first, count, cols)
                received = [packed[0]] + [lax.ppermute(packed[d], "wide", routes[d]) for d in range(1, chips)]
                sent.append((received, first, count))
            acc = jnp.zeros((slab_rows, ROWCAP), F32)
            for received, first, count in sent:
                acc = contract_chunk(table, received, integrals, spread, (big, mask_a, mask_b), acc, first, count)
            own, other = split(table, acc, column_class, chips, cap_back)
            halves = add_cores(own, lax.ppermute(other, "wide", swap))
            back = [halves[0]] + [lax.ppermute(halves[d], "wide", routes[d]) for d in range(1, chips)]
            slab_energy = (vir_energy[: slab_rows // nvir, None] + vir_energy[None, :]).reshape(1, -1)
            pair_energy = (occ_energy[:, None] + occ_energy[None, :]).reshape(-1)
            own_energy = lax.dynamic_slice_in_dim(pair_energy, position * pairs_local, pairs_local, 0)
            return finish(table, back, own_energy, column_class, slab_energy)

        return run

    def dense_plan(amplitudes, integrals, early):
        return dense_body(amplitudes, integrals, *given[2:])

    plans = [compact_plan(n, m) for n, m in LEVELS] + [dense_plan]
    return lax.switch(level, plans, amplitudes, integrals, early)


def solution(mesh):
    return jax.shard_map(
        body,
        mesh=mesh,
        in_specs=(
            P(("parts", "wide"), None),
            P("parts", "wide"),
            P("parts"),
            P("parts"),
            P("parts"),
            P("parts"),
        ),
        out_specs=P(("parts", "wide"), None),
        check_vma=False,
    )
```

```python
import jax
import jax.numpy as jnp
from jax import lax
from jax.experimental import pallas as pl
from jax.experimental.pallas import tpu as pltpu
from jax.sharding import PartitionSpec as P

BLK = 64
LANE = 128
SUB = 8
NBLK = 8
CORES = 2
ROWCAP = 256
CHUNKS = ((0, 8), (16, 16), (8, 8))
LEVELS = ((96, 24), (112, 24), (144, 24))
MOST = max(cap for cap, _ in LEVELS)
CHIP, CORE, PURE, TILE_A, TILE_B, ROLL, TILE_U, TILE_W, HALF, KIND, ROLE, LEVEL, SLAB = 0, 1, 2, 4, 5, 6, 7, 8, 9, 16, 24, 27, 28
START, COUNT, ROW_CLASS, ROW_RANK, SIZE = 32, 96, 128, 192, 256
TYPES = ((0, 1, 2), (1, 0, 3), (2, 3, 0))
SMEM = pltpu.SMEM
VMEM = pltpu.VMEM
GRANT = 48 * 1024 * 1024
BF = jnp.bfloat16
F32 = jnp.float32
I32 = jnp.int32


def block_lookup(table, block_ids):
    labels = jnp.arange(table.shape[0], dtype=jnp.int32)
    hits = block_ids[:, None] == labels[None, :]
    return jnp.sum(jnp.where(hits, table[None, :], 0), axis=1)


def contract(left, right):
    return lax.dot_general(
        left, right, (((1,), (1,)), ((), ())), preferred_element_type=jnp.float32
    )


def dense_body(amplitudes, integrals, occ_irrep, vir_irrep, occ_energy, vir_energy):
    position = lax.axis_index("wide")
    pairs_local = amplitudes.shape[0]
    local_cols = integrals.shape[1]
    nvir = vir_energy.shape[0]
    slab_rows = integrals.shape[0]
    slab_first = slab_rows // nvir
    gathered = lax.all_to_all(amplitudes, "wide", split_axis=1, concat_axis=0, tiled=True)
    flat_cols = position * local_cols + jnp.arange(local_cols, dtype=jnp.int32)
    first_vir = flat_cols // nvir
    second_vir = flat_cols % nvir
    col_irrep = jnp.bitwise_xor(
        block_lookup(vir_irrep, first_vir // BLK), block_lookup(vir_irrep, second_vir // BLK)
    )
    vir_label = block_lookup(vir_irrep, jnp.arange(nvir, dtype=jnp.int32) // BLK)
    pair_irrep = jnp.bitwise_xor(occ_irrep[:, None], occ_irrep[None, :]).reshape(-1)
    slab_irrep = jnp.bitwise_xor(vir_label[:slab_first, None], vir_label[None, :]).reshape(-1)
    kept_t = jnp.where(pair_irrep[:, None] == col_irrep[None, :], gathered, 0)
    kept_v = jnp.where(slab_irrep[:, None] == col_irrep[None, :], integrals, 0)
    summed = lax.psum_scatter(contract(kept_t, kept_v), "wide", scatter_dimension=0, tiled=True)
    slab_energy = (vir_energy[:slab_first, None] + vir_energy[None, :]).reshape(-1)
    pair_energy = (occ_energy[:, None] + occ_energy[None, :]).reshape(-1)
    local_pair_energy = lax.dynamic_slice_in_dim(
        pair_energy, position * pairs_local, pairs_local, 0
    )
    denominator = slab_energy[None, :] - local_pair_energy[:, None]
    return summed / denominator


def tile(ref, lead, c, which):
    start = pl.multiple_of(c * NBLK * BLK + which * LANE, LANE)
    return ref[lead + (slice(None), pl.ds(start, LANE))]


def maybe_roll(x, flag):
    return jnp.where(flag == 1, jnp.concatenate([x[:, BLK:], x[:, :BLK]], axis=1), x)


def half_masks(table, shape):
    half = (lax.broadcasted_iota(I32, shape, 1) % LANE) // BLK
    first = half == table[HALF]
    return jnp.where(first, 1.0, 0.0).astype(BF), jnp.where(first, 0.0, 1.0).astype(BF)


def setup_kernel(
    devices, nslab, place, occ, vir, occ_here, occ_lane, occ_rows, table, pick_ref, big_ref, a_ref, b_ref, class_ref, hist, tally
):
    chips = devices // CORES
    nocc = occ.shape[0]
    per_device = nocc // devices
    chip, core = place[0], place[1]
    table[CHIP] = chip
    table[CORE] = core
    common, zero_at, seven_at = vir[0] * 0, vir[0] * 0, vir[0] * 0
    for b in range(NBLK):
        label = vir[b]
        common = jnp.where((label != 0) & (label != 7), label, common)
        zero_at = jnp.where(label == 0, b, zero_at)
        seven_at = jnp.where(label == 7, b, seven_at)
        table[KIND + b] = jnp.where(label == 0, 1, jnp.where(label == 7, 2, 0))
    irreps = [common * 0, common, common ^ 7, common * 0 + 7]
    needed = []
    for g in range(4):
        some = common * 0
        for b in range(NBLK):
            some = jnp.where((vir[0] ^ vir[b]) == irreps[g], 1, some)
        needed.append(some)

    tile_a, half_a = zero_at // 2, zero_at % 2
    same = seven_at // 2 == tile_a
    tile_b = jnp.where(same, (tile_a + 1) % 4, seven_at // 2)
    pure = jnp.where((tile_a != 0) & (tile_b != 0), 0, jnp.where((tile_a != 1) & (tile_b != 1), 1, 2))
    table[PURE] = pure
    table[PURE + 1] = 6 - tile_a - tile_b - pure
    table[TILE_A] = tile_a
    table[TILE_B] = tile_b
    table[ROLL] = jnp.where(same | (seven_at % 2 != half_a), 0, 1)
    table[TILE_U] = jnp.where(same, tile_a, tile_b)
    table[TILE_W] = jnp.where(same, tile_b, tile_a)
    table[HALF] = half_a

    for h in range(NBLK):
        hist[h] = 0
    for j in range(nocc):
        hist[NBLK + j] = hist[occ[j]]
        hist[occ[j]] = hist[occ[j]] + 1
    of_i = lambda i, g: hist[occ[i] ^ irreps[g]] * needed[g]
    biggest = common * 0
    most_class = common * 0
    for g in range(4):
        total = common * 0
        for s in range(devices):
            table[START + g * devices + s] = total
            here = common * 0
            for i in range(per_device):
                here += of_i(s * per_device + i, g)
            total += here
            biggest = jnp.maximum(biggest, here)
            tally[g * devices + s] = here
        most_class = jnp.maximum(most_class, total)
        for c in range(chips):
            table[COUNT + g * chips + c] = tally[g * devices + c * CORES] + tally[g * devices + c * CORES + 1]
    most = common * 0
    for c in range(chips):
        n = [table[COUNT + g * chips + c] for g in range(4)]
        for b, a, s in TYPES:
            most = jnp.maximum(most, 3 * n[b] + jnp.maximum(n[a], n[s]))
    level = common * 0 + len(LEVELS)
    for at in range(len(LEVELS) - 1, -1, -1):
        cap, cap_back = LEVELS[at]
        level = jnp.where((most <= cap) & (biggest <= cap_back) & (most_class <= ROWCAP), at, level)
    table[LEVEL] = level

    roles_of = lambda kind: [jnp.where(kind == 0, x, jnp.where(kind == 1, y, z)) for x, y, z in zip(*TYPES)]
    roles, of_slab = roles_of(table[KIND + chip]), roles_of(table[KIND])
    for n in range(3):
        table[ROLE + n] = roles[n]
        table[SLAB + n] = of_slab[n]
    position = chip * CORES + core
    for i in range(per_device):
        at = position * per_device + i
        for j in range(nocc):
            both = occ[at] ^ occ[j]
            kind = common * 0 + 4
            rank = hist[NBLK + j]
            for g in range(4):
                hit = (both == irreps[g]) & (needed[g] == 1)
                kind = jnp.where(hit, g, kind)
                for before in range(i):
                    rank = rank + jnp.where(hit, of_i(position * per_device + before, g), 0)
            table[ROW_CLASS + i * nocc + j] = kind
            table[ROW_RANK + i * nocc + j] = rank

    width = CORES * per_device * nocc
    lane = lax.broadcasted_iota(I32, (1, width), 1)
    earlier = lax.broadcasted_iota(I32, (nocc, width), 0) < lax.broadcasted_iota(I32, (nocc, width), 1) % nocc
    alike = jnp.where((occ_rows[...] == occ_lane[...]) & earlier, 1, 0)
    rank = jnp.sum(alike, axis=0, keepdims=True)
    irrep = occ_lane[...] ^ occ_here[...]
    spots = []
    for g in range(4):
        base, run = jnp.zeros((1, width), I32), common * 0
        for i in range(CORES * per_device):
            shown = i ^ (core * per_device)
            base = jnp.where(lane // nocc == shown, run, base)
            run += of_i(chip * CORES * per_device + i, g)
        spots.append((jnp.where((irrep == irreps[g]) & (needed[g] == 1), base + rank, -4 * MOST), run))
    slot = lax.broadcasted_iota(I32, (MOST, width), 0)
    for t, (b, a, s) in enumerate(TYPES):
        for section, (g, f) in enumerate(((b, 0), (b, 1), (b, 2), (a, 3), (s, 3))):
            target = spots[g][0] + f * spots[b][1]
            pick_ref[t, :, section * width : (section + 1) * width] = jnp.where(slot == target, 1.0, 0.0).astype(BF)

    half = lax.broadcasted_iota(I32, (BLK, LANE), 1) // BLK == half_a
    column = lax.broadcasted_iota(I32, class_ref.shape, 1) % (NBLK * BLK) // BLK
    column_class = jnp.zeros(class_ref.shape, I32)
    for b in range(NBLK):
        both = vir[0] ^ vir[b]
        kind = common * 0 + 4
        for g in range(4):
            kind = jnp.where(both == irreps[g], g, kind)
        column_class = jnp.where(column == b, kind, column_class)
        is_ = [jnp.where(kind == roles[n], 1.0, 0.0) for n in range(3)]
        full = jnp.zeros((BLK, LANE), F32)
        for a in range(nslab):
            rows = slice((a * NBLK + b) * BLK, (a * NBLK + b + 1) * BLK)
            big_ref[rows, :] = (full + is_[0]).astype(BF)
            a_ref[rows, :] = jnp.where(half, full + is_[1], 0.0).astype(BF)
            b_ref[rows, :] = jnp.where(half, 0.0, full + is_[2]).astype(BF)
    class_ref[...] = column_class


def setup(place, occ, vir, slab_rows, devices):
    nocc = occ.shape[0]
    width = CORES * nocc // devices * nocc
    per_chip = width // nocc
    chip, core = place[0], place[1]
    mine = lax.dynamic_slice_in_dim(occ, chip * per_chip, per_chip, 0).reshape(CORES, -1)
    mine = jnp.where(core == 0, mine, mine[::-1]).reshape(-1)
    occ_here = jnp.repeat(mine, nocc)[None, :]
    occ_lane = jnp.tile(occ, per_chip)[None, :]
    occ_rows = jnp.broadcast_to(occ[:, None], (nocc, width))
    smem, vmem = pl.BlockSpec(memory_space=SMEM), pl.BlockSpec(memory_space=VMEM)
    mask = jax.ShapeDtypeStruct((slab_rows, LANE), BF)
    return pl.pallas_call(
        lambda *refs: setup_kernel(devices, slab_rows // (NBLK * BLK), *refs),
        in_specs=[smem] * 3 + [vmem] * 3,
        out_specs=[smem] + [vmem] * 5,
        out_shape=[
            jax.ShapeDtypeStruct((SIZE,), I32),
            jax.ShapeDtypeStruct((3, MOST, 5 * width), BF),
            mask,
            mask,
            mask,
            jax.ShapeDtypeStruct((1, slab_rows), I32),
        ],
        scratch_shapes=[SMEM((NBLK + nocc,), I32), SMEM((4 * devices,), I32)],
        name="setup",
    )(place, occ, vir, occ_here, occ_lane, occ_rows)


def cost(micros):
    return pl.CostEstimate(flops=0, bytes_accessed=int(micros * 3_690_000), transcendentals=0)


def take_kernel(chips, table, *refs):
    for d in range(chips):
        refs[chips][d] = refs[d][...]


def take_for_sibling(table, amplitudes, first, count, cols_device):
    rows, width = amplitudes.shape[0], count * NBLK * BLK
    chips = amplitudes.shape[1] // cols_device // CORES
    step = 2 * NBLK * BLK
    per_device = cols_device // step

    def column(d):
        return lambda q, s: (0, (d * CORES + 1 - s[CORE]) * per_device + first // 2 + q)

    return pl.pallas_call(
        lambda *refs: take_kernel(chips, *refs),
        grid_spec=pltpu.PrefetchScalarGridSpec(
            num_scalar_prefetch=1,
            grid=(width // step,),
            in_specs=[pl.BlockSpec((rows, step), column(d)) for d in range(chips)],
            out_specs=pl.BlockSpec((chips, rows, step), lambda q, s: (0, 0, q)),
        ),
        out_shape=jax.ShapeDtypeStruct((chips, rows, width), amplitudes.dtype),
        cost_estimate=cost(1.5 + 0.5 * count),
        name="take_for_sibling",
    )(table, *[amplitudes] * chips)


def pack_kernel(count, table, own_ref, sib_ref, pick_ref, out_ref):
    pick = pick_ref[0]
    mine, other = half_masks(table, (own_ref.shape[0], LANE))

    def pair(u, carry):
        columns = []
        for c in (2 * u, 2 * u + 1):
            parts = [[], [], [], [], []]
            for ref, lead in ((own_ref, ()), (sib_ref, (0,))):
                at = lambda n: tile(ref, lead, c, table[n])
                parts[0].append(at(PURE))
                parts[1].append(at(PURE + 1))
                parts[2].append(at(TILE_W) * other + maybe_roll(at(TILE_B), table[ROLL]) * mine)
                parts[3].append(at(TILE_A) * mine)
                parts[4].append(maybe_roll(at(TILE_U), table[ROLL]) * other)
            columns.append(jnp.concatenate([x for part in parts for x in part], axis=0))
        rows = jnp.concatenate(columns, axis=1)
        lanes = pl.ds(pl.multiple_of(u * 2 * LANE, 2 * LANE), 2 * LANE)
        out_ref[0, :, lanes] = jnp.dot(pick, rows, preferred_element_type=F32).astype(BF)
        return carry

    lax.fori_loop(0, count // 2, pair, 0)


def pack(table, amplitudes, sibling, pick, cap, first, count, cols_device):
    rows, width = amplitudes.shape[0], count * NBLK * BLK
    chips = amplitudes.shape[1] // cols_device // CORES
    per_device = cols_device // width

    def column(d, s):
        return (0, (d * CORES + s[CORE]) * per_device + first // count)

    out = jax.ShapeDtypeStruct((chips, cap, count * LANE), BF)
    return pl.pallas_call(
        lambda *refs: pack_kernel(count, *refs),
        grid_spec=pltpu.PrefetchScalarGridSpec(
            num_scalar_prefetch=1,
            grid=(chips,),
            in_specs=[
                pl.BlockSpec((rows, width), column),
                pl.BlockSpec((1, rows, width), lambda d, s: (d, 0, 0)),
                pl.BlockSpec((1, cap, pick.shape[2]), lambda d, s: (s[KIND + d], 0, 0)),
            ],
            out_specs=pl.BlockSpec((1, cap, count * LANE), lambda d, s: (d, 0, 0)),
        ),
        out_shape=out,
        compiler_params=pltpu.CompilerParams(vmem_limit_bytes=GRANT),
        cost_estimate=cost(4 + 0.65 * count),
        name="pack",
    )(table, amplitudes, sibling, pick)


def spread_kernel(chips, cap, table, spread_ref):
    column = lax.broadcasted_iota(I32, (1, chips * cap), 1)
    row = lax.broadcasted_iota(I32, (ROWCAP, chips * cap), 0)
    for section, (n, f) in enumerate(((0, 0), (0, 1), (0, 2), (1, 3), (2, 3))):
        target = jnp.full((1, chips * cap), -1, I32)
        for d in range(chips):
            chip = d
            group = table[ROLE + n]
            k = column - d * cap - f * table[COUNT + table[ROLE] * chips + chip]
            count = table[COUNT + group * chips + chip]
            start = table[START + (group * chips + chip) * CORES]
            inside = (column >= d * cap) & (column < (d + 1) * cap) & (k >= 0) & (k < count)
            target = jnp.where(inside, start + k, target)
        spread_ref[section * ROWCAP : (section + 1) * ROWCAP, :] = jnp.where(row == target, 1.0, 0.0).astype(BF)


def make_spread(table, chips, cap):
    return pl.pallas_call(
        lambda *refs: spread_kernel(chips, cap, *refs),
        in_specs=[pl.BlockSpec(memory_space=SMEM)],
        out_specs=pl.BlockSpec(memory_space=VMEM),
        out_shape=jax.ShapeDtypeStruct((5 * ROWCAP, chips * cap), BF),
        compiler_params=pltpu.CompilerParams(vmem_limit_bytes=GRANT),
        cost_estimate=cost(1),
        name="make_spread",
    )(table)


def contract_kernel(table, got_ref, vals, spread_ref, big_ref, a_ref, b_ref, acc_ref, out_ref):

    @pl.when(pl.program_id(0) == 0)
    def _():
        out_ref[...] = acc_ref[...]

    received = got_ref[...].reshape(-1, got_ref.shape[2])
    spread = jnp.dot(spread_ref[...], received, preferred_element_type=F32)
    left = [spread[j * ROWCAP : (j + 1) * ROWCAP] for j in range(5)]
    half = (lax.broadcasted_iota(I32, (ROWCAP, 2 * LANE), 1) % LANE) // BLK
    left = [x.astype(BF) for x in left[:3] + [jnp.where(half == table[HALF], left[3], left[4])]]
    mine, other = half_masks(table, (vals.shape[0], LANE))
    right = [[], [], [], []]
    for c in (0, 1):
        at = lambda n: tile(vals, (), c, table[n])
        right[0].append(at(PURE) * big_ref[...])
        right[1].append(at(PURE + 1) * big_ref[...])
        right[2].append((at(TILE_W) * other + maybe_roll(at(TILE_B), table[ROLL]) * mine) * big_ref[...])
        right[3].append(at(TILE_A) * a_ref[...] + maybe_roll(at(TILE_U), table[ROLL]) * b_ref[...])
    right = jnp.concatenate([x for part in right for x in part], axis=1)
    out_ref[...] += contract(right, jnp.concatenate(left, axis=1))


def contract_chunk(table, received, integrals, spread, masks, acc, first, count):
    chips, cap = received.shape[:2]
    slab = integrals.shape[0]
    fixed = lambda u, s: (0, 0)
    return pl.pallas_call(
        contract_kernel,
        grid_spec=pltpu.PrefetchScalarGridSpec(
            num_scalar_prefetch=1,
            grid=(count // 2,),
            in_specs=[pl.BlockSpec((chips, cap, 2 * LANE), lambda u, s: (0, 0, u))]
            + [pl.BlockSpec((slab, 2 * NBLK * BLK), lambda u, s: (0, first // 2 + u))]
            + [pl.BlockSpec(x.shape, fixed) for x in (spread, *masks, acc)],
            out_specs=pl.BlockSpec(acc.shape, fixed),
        ),
        out_shape=jax.ShapeDtypeStruct(acc.shape, F32),
        compiler_params=pltpu.CompilerParams(vmem_limit_bytes=GRANT),
        cost_estimate=cost(1.5 + 1.3 * count),
        name="contract_chunk",
    )(table, received, integrals, spread, *masks, acc)


def split_kernel(chips, cap, table, sums_ref, class_ref, own_ref, sib_ref, held):
    d = pl.program_id(0)

    @pl.when(d == 0)
    def _():
        held[:ROWCAP, :] = sums_ref[...].T
        held[ROWCAP:, :] = jnp.zeros((cap + SUB, held.shape[1]), F32)

    kind = class_ref[...]
    for flip, ref in ((0, own_ref), (1, sib_ref)):
        device = d * CORES + (table[CORE] ^ flip)
        rows = []
        for n in range(3):
            start = table[START + table[SLAB + n] * chips * CORES + device]
            odd = start % SUB
            window = held[pl.ds(pl.multiple_of(start - odd, SUB), cap + SUB), :]
            rows.append(pltpu.roll(window, (cap + SUB - odd) % (cap + SUB), 0)[:cap])
        ref[0] = jnp.where(kind == table[SLAB], rows[0], jnp.where(kind == table[SLAB + 1], rows[1], rows[2]))


def split(table, sums, column_class, chips, cap):
    slab = sums.shape[0]
    out = jax.ShapeDtypeStruct((chips, cap, slab), F32)
    fixed = lambda d, s: (0, 0)
    return pl.pallas_call(
        lambda *refs: split_kernel(chips, cap, *refs),
        grid_spec=pltpu.PrefetchScalarGridSpec(
            num_scalar_prefetch=1,
            grid=(chips,),
            in_specs=[pl.BlockSpec(sums.shape, fixed), pl.BlockSpec((1, slab), fixed)],
            out_specs=[pl.BlockSpec((1, cap, slab), lambda d, s: (d, 0, 0))] * 2,
            scratch_shapes=[pltpu.VMEM((ROWCAP + cap + SUB, slab), F32)],
        ),
        out_shape=[out, out],
        cost_estimate=cost(6),
        name="split_sums",
    )(table, sums, column_class)


def finish_kernel(pairs, table, energies, class_ref, slab_ref, parts, out_ref, held):
    total = parts[0]
    for n in range(1, parts.shape[0]):
        total = total + parts[n]
    held[...] = total

    def one(p, carry):
        kind = table[ROW_CLASS + p]
        row = held[pl.ds(jnp.where(kind < 4, table[ROW_RANK + p], 0), 1), :]
        kept = jnp.where(class_ref[...] == kind, row, 0.0)
        out_ref[pl.ds(p, 1), :] = kept / (slab_ref[...] - energies[p])
        return carry

    lax.fori_loop(0, pairs, one, 0)


def finish(table, parts, energies, column_class, slab_energy):
    pairs, slab = energies.shape[0], column_class.shape[1]
    smem, vmem = pl.BlockSpec(memory_space=SMEM), pl.BlockSpec(memory_space=VMEM)
    return pl.pallas_call(
        lambda *refs: finish_kernel(pairs, *refs),
        in_specs=[smem] * 2 + [vmem] * 3,
        out_specs=vmem,
        out_shape=jax.ShapeDtypeStruct((pairs, slab), F32),
        scratch_shapes=[pltpu.VMEM(parts.shape[1:], F32)],
        cost_estimate=pl.CostEstimate(flops=4 * pairs * slab, bytes_accessed=8 * pairs * slab, transcendentals=0),
        name="finish",
    )(table, energies, column_class, slab_energy, parts)


def body(amplitudes, integrals, occ_irrep, vir_irrep, occ_energy, vir_energy):
    devices = lax.axis_size("wide")
    pairs_local = amplitudes.shape[0]
    cols = integrals.shape[1]
    slab_rows = integrals.shape[0]
    nvir = vir_energy.shape[0]
    nocc = occ_irrep.shape[0]
    given = (amplitudes, integrals, occ_irrep, vir_irrep, occ_energy, vir_energy)
    compact = (
        nvir == NBLK * BLK
        and CORES * cols == BLK * nvir
        and cols == sum(count for _, count in CHUNKS) * nvir
        and pairs_local % 16 == 0
        and devices == 16
        and nocc == 32
        and devices * pairs_local == nocc * nocc
        and lax.axis_size("parts") == 2
    )
    if not compact:
        return dense_body(*given)

    chips = devices // CORES
    position = lax.axis_index("wide")
    place = jnp.stack([position // CORES, position % CORES]).astype(I32)
    swap = [(i, i ^ 1) for i in range(devices)]
    cores = [list(range(core, devices, CORES)) for core in range(CORES)]

    def exchange(x):
        return lax.all_to_all(x, "wide", 0, 0, axis_index_groups=cores, tiled=True)

    table, pick, big, mask_a, mask_b, column_class = setup(place, occ_irrep, vir_irrep, slab_rows, devices)
    level = table[LEVEL : LEVEL + 1]
    level = jnp.maximum(level, lax.ppermute(level, "parts", [(0, 1), (1, 0)]))[0]

    def take(n, after=None):
        at = place if after is None else lax.optimization_barrier((place, after))[0]
        return take_for_sibling(at, amplitudes, *CHUNKS[n], cols)

    first_take = take(0)
    early = (lax.ppermute(first_take, "wide", swap), take(1, first_take))

    def compact_plan(cap, cap_back):
        def run(amplitudes, integrals, early):
            spread = make_spread(table, chips, cap)
            sent = []
            siblings = [early[0], lax.ppermute(early[1], "wide", swap)]
            acc = jnp.zeros((slab_rows, ROWCAP), F32)
            received = []
            for n, (first, count) in enumerate(CHUNKS):
                packed = pack(table, amplitudes, siblings[n], pick, cap, first, count, cols)
                if n + 2 < len(CHUNKS):
                    siblings.append(lax.ppermute(take(n + 2, packed), "wide", swap))
                received.append(exchange(packed))
            for n, (first, count) in enumerate(CHUNKS):
                acc = contract_chunk(table, received[n], integrals, spread, (big, mask_a, mask_b), acc, first, count)
            own, other = split(table, acc, column_class, chips, cap_back)
            back = exchange(own + lax.ppermute(other, "wide", swap))
            slab_energy = (vir_energy[: slab_rows // nvir, None] + vir_energy[None, :]).reshape(1, -1)
            pair_energy = (occ_energy[:, None] + occ_energy[None, :]).reshape(-1)
            own_energy = lax.dynamic_slice_in_dim(pair_energy, position * pairs_local, pairs_local, 0)
            return finish(table, back, own_energy, column_class, slab_energy)

        return run

    def dense_plan(amplitudes, integrals, early):
        return dense_body(amplitudes, integrals, *given[2:])

    plans = [compact_plan(n, m) for n, m in LEVELS] + [dense_plan]
    usual = lambda *held: lax.switch(level, plans[:2], *held)
    rare = lambda *held: lax.switch(level - 2, plans[2:], *held)
    return lax.cond(level < 2, usual, rare, amplitudes, integrals, early)


def solution(mesh):
    return jax.shard_map(
        body,
        mesh=mesh,
        in_specs=(
            P(("parts", "wide"), None),
            P("parts", "wide"),
            P("parts"),
            P("parts"),
            P("parts"),
            P("parts"),
        ),
        out_specs=P(("parts", "wide"), None),
        check_vma=False,
    )
```

```python
import jax
import jax.numpy as jnp
from jax import lax
from jax.experimental import pallas as pl
from jax.experimental.pallas import tpu as pltpu
from jax.sharding import PartitionSpec as P

BLK = 64
LANE = 128
SUB = 8
NBLK = 8
CORES = 2
ROWCAP = 256
CHUNKS = ((0, 8), (16, 16), (8, 8))
LEVELS = ((96, 24), (112, 24), (144, 24))
MOST = max(cap for cap, _ in LEVELS)
CHIP, CORE, PURE, TILE_A, TILE_B, ROLL, TILE_U, TILE_W, HALF, KIND, ROLE, LEVEL, SLAB = 0, 1, 2, 4, 5, 6, 7, 8, 9, 16, 24, 27, 28
START, COUNT, ROW_CLASS, ROW_RANK, SIZE = 32, 96, 128, 192, 256
TYPES = ((0, 1, 2), (1, 0, 3), (2, 3, 0))
SMEM = pltpu.SMEM
VMEM = pltpu.VMEM
GRANT = 48 * 1024 * 1024
BF = jnp.bfloat16
F32 = jnp.float32
I32 = jnp.int32


def block_lookup(table, block_ids):
    labels = jnp.arange(table.shape[0], dtype=jnp.int32)
    hits = block_ids[:, None] == labels[None, :]
    return jnp.sum(jnp.where(hits, table[None, :], 0), axis=1)


def contract(left, right):
    return lax.dot_general(
        left, right, (((1,), (1,)), ((), ())), preferred_element_type=jnp.float32
    )


def dense_body(amplitudes, integrals, occ_irrep, vir_irrep, occ_energy, vir_energy):
    position = lax.axis_index("wide")
    pairs_local = amplitudes.shape[0]
    local_cols = integrals.shape[1]
    nvir = vir_energy.shape[0]
    slab_rows = integrals.shape[0]
    slab_first = slab_rows // nvir
    gathered = lax.all_to_all(amplitudes, "wide", split_axis=1, concat_axis=0, tiled=True)
    flat_cols = position * local_cols + jnp.arange(local_cols, dtype=jnp.int32)
    first_vir = flat_cols // nvir
    second_vir = flat_cols % nvir
    col_irrep = jnp.bitwise_xor(
        block_lookup(vir_irrep, first_vir // BLK), block_lookup(vir_irrep, second_vir // BLK)
    )
    vir_label = block_lookup(vir_irrep, jnp.arange(nvir, dtype=jnp.int32) // BLK)
    pair_irrep = jnp.bitwise_xor(occ_irrep[:, None], occ_irrep[None, :]).reshape(-1)
    slab_irrep = jnp.bitwise_xor(vir_label[:slab_first, None], vir_label[None, :]).reshape(-1)
    kept_t = jnp.where(pair_irrep[:, None] == col_irrep[None, :], gathered, 0)
    kept_v = jnp.where(slab_irrep[:, None] == col_irrep[None, :], integrals, 0)
    summed = lax.psum_scatter(contract(kept_t, kept_v), "wide", scatter_dimension=0, tiled=True)
    slab_energy = (vir_energy[:slab_first, None] + vir_energy[None, :]).reshape(-1)
    pair_energy = (occ_energy[:, None] + occ_energy[None, :]).reshape(-1)
    local_pair_energy = lax.dynamic_slice_in_dim(
        pair_energy, position * pairs_local, pairs_local, 0
    )
    denominator = slab_energy[None, :] - local_pair_energy[:, None]
    return summed / denominator


def tile(ref, lead, c, which):
    start = pl.multiple_of(c * NBLK * BLK + which * LANE, LANE)
    return ref[lead + (slice(None), pl.ds(start, LANE))]


def maybe_roll(x, flag):
    return jnp.where(flag == 1, jnp.concatenate([x[:, BLK:], x[:, :BLK]], axis=1), x)


def half_masks(table, shape):
    half = (lax.broadcasted_iota(I32, shape, 1) % LANE) // BLK
    first = half == table[HALF]
    return jnp.where(first, 1.0, 0.0).astype(BF), jnp.where(first, 0.0, 1.0).astype(BF)


def setup_kernel(
    devices, nslab, place, occ, vir, occ_here, occ_lane, occ_rows, table, pick_ref, big_ref, a_ref, b_ref, class_ref, hist, tally
):
    chips = devices // CORES
    nocc = occ.shape[0]
    per_device = nocc // devices
    chip, core = place[0], place[1]
    table[CHIP] = chip
    table[CORE] = core
    common, zero_at, seven_at = vir[0] * 0, vir[0] * 0, vir[0] * 0
    for b in range(NBLK):
        label = vir[b]
        common = jnp.where((label != 0) & (label != 7), label, common)
        zero_at = jnp.where(label == 0, b, zero_at)
        seven_at = jnp.where(label == 7, b, seven_at)
        table[KIND + b] = jnp.where(label == 0, 1, jnp.where(label == 7, 2, 0))
    irreps = [common * 0, common, common ^ 7, common * 0 + 7]
    needed = []
    for g in range(4):
        some = common * 0
        for b in range(NBLK):
            some = jnp.where((vir[0] ^ vir[b]) == irreps[g], 1, some)
        needed.append(some)

    tile_a, half_a = zero_at // 2, zero_at % 2
    same = seven_at // 2 == tile_a
    tile_b = jnp.where(same, (tile_a + 1) % 4, seven_at // 2)
    pure = jnp.where((tile_a != 0) & (tile_b != 0), 0, jnp.where((tile_a != 1) & (tile_b != 1), 1, 2))
    table[PURE] = pure
    table[PURE + 1] = 6 - tile_a - tile_b - pure
    table[TILE_A] = tile_a
    table[TILE_B] = tile_b
    table[ROLL] = jnp.where(same | (seven_at % 2 != half_a), 0, 1)
    table[TILE_U] = jnp.where(same, tile_a, tile_b)
    table[TILE_W] = jnp.where(same, tile_b, tile_a)
    table[HALF] = half_a

    for h in range(NBLK):
        hist[h] = 0
    for j in range(nocc):
        hist[NBLK + j] = hist[occ[j]]
        hist[occ[j]] = hist[occ[j]] + 1
    of_i = lambda i, g: hist[occ[i] ^ irreps[g]] * needed[g]
    biggest = common * 0
    most_class = common * 0
    for g in range(4):
        total = common * 0
        for s in range(devices):
            table[START + g * devices + s] = total
            here = common * 0
            for i in range(per_device):
                here += of_i(s * per_device + i, g)
            total += here
            biggest = jnp.maximum(biggest, here)
            tally[g * devices + s] = here
        most_class = jnp.maximum(most_class, total)
        for c in range(chips):
            table[COUNT + g * chips + c] = tally[g * devices + c * CORES] + tally[g * devices + c * CORES + 1]
    most = common * 0
    for c in range(chips):
        n = [table[COUNT + g * chips + c] for g in range(4)]
        for b, a, s in TYPES:
            most = jnp.maximum(most, 3 * n[b] + jnp.maximum(n[a], n[s]))
    level = common * 0 + len(LEVELS)
    for at in range(len(LEVELS) - 1, -1, -1):
        cap, cap_back = LEVELS[at]
        level = jnp.where((most <= cap) & (biggest <= cap_back) & (most_class <= ROWCAP), at, level)
    table[LEVEL] = level

    roles_of = lambda kind: [jnp.where(kind == 0, x, jnp.where(kind == 1, y, z)) for x, y, z in zip(*TYPES)]
    roles, of_slab = roles_of(table[KIND + chip]), roles_of(table[KIND])
    for n in range(3):
        table[ROLE + n] = roles[n]
        table[SLAB + n] = of_slab[n]
    position = chip * CORES + core
    for i in range(per_device):
        at = position * per_device + i
        for j in range(nocc):
            both = occ[at] ^ occ[j]
            kind = common * 0 + 4
            rank = hist[NBLK + j]
            for g in range(4):
                hit = (both == irreps[g]) & (needed[g] == 1)
                kind = jnp.where(hit, g, kind)
                for before in range(i):
                    rank = rank + jnp.where(hit, of_i(position * per_device + before, g), 0)
            table[ROW_CLASS + i * nocc + j] = kind
            table[ROW_RANK + i * nocc + j] = rank

    width = CORES * per_device * nocc
    lane = lax.broadcasted_iota(I32, (1, width), 1)
    earlier = lax.broadcasted_iota(I32, (nocc, width), 0) < lax.broadcasted_iota(I32, (nocc, width), 1) % nocc
    alike = jnp.where((occ_rows[...] == occ_lane[...]) & earlier, 1, 0)
    rank = jnp.sum(alike, axis=0, keepdims=True)
    irrep = occ_lane[...] ^ occ_here[...]
    spots = []
    for g in range(4):
        base, run = jnp.zeros((1, width), I32), common * 0
        for i in range(CORES * per_device):
            shown = i ^ (core * per_device)
            base = jnp.where(lane // nocc == shown, run, base)
            run += of_i(chip * CORES * per_device + i, g)
        spots.append((jnp.where((irrep == irreps[g]) & (needed[g] == 1), base + rank, -4 * MOST), run))
    slot = lax.broadcasted_iota(I32, (MOST, width), 0)
    for t, (b, a, s) in enumerate(TYPES):
        for section, (g, f) in enumerate(((b, 0), (b, 1), (b, 2), (a, 3), (s, 3))):
            target = spots[g][0] + f * spots[b][1]
            pick_ref[t, :, section * width : (section + 1) * width] = jnp.where(slot == target, 1.0, 0.0).astype(BF)

    half = lax.broadcasted_iota(I32, (BLK, LANE), 1) // BLK == half_a
    column = lax.broadcasted_iota(I32, class_ref.shape, 1) % (NBLK * BLK) // BLK
    column_class = jnp.zeros(class_ref.shape, I32)
    for b in range(NBLK):
        both = vir[0] ^ vir[b]
        kind = common * 0 + 4
        for g in range(4):
            kind = jnp.where(both == irreps[g], g, kind)
        column_class = jnp.where(column == b, kind, column_class)
        is_ = [jnp.where(kind == roles[n], 1.0, 0.0) for n in range(3)]
        full = jnp.zeros((BLK, LANE), F32)
        for a in range(nslab):
            rows = slice((a * NBLK + b) * BLK, (a * NBLK + b + 1) * BLK)
            big_ref[rows, :] = (full + is_[0]).astype(BF)
            a_ref[rows, :] = jnp.where(half, full + is_[1], 0.0).astype(BF)
            b_ref[rows, :] = jnp.where(half, 0.0, full + is_[2]).astype(BF)
    class_ref[...] = column_class


def setup(place, occ, vir, slab_rows, devices):
    nocc = occ.shape[0]
    width = CORES * nocc // devices * nocc
    per_chip = width // nocc
    chip, core = place[0], place[1]
    mine = lax.dynamic_slice_in_dim(occ, chip * per_chip, per_chip, 0).reshape(CORES, -1)
    mine = jnp.where(core == 0, mine, mine[::-1]).reshape(-1)
    occ_here = jnp.repeat(mine, nocc)[None, :]
    occ_lane = jnp.tile(occ, per_chip)[None, :]
    occ_rows = jnp.broadcast_to(occ[:, None], (nocc, width))
    smem, vmem = pl.BlockSpec(memory_space=SMEM), pl.BlockSpec(memory_space=VMEM)
    mask = jax.ShapeDtypeStruct((slab_rows, LANE), BF)
    return pl.pallas_call(
        lambda *refs: setup_kernel(devices, slab_rows // (NBLK * BLK), *refs),
        in_specs=[smem] * 3 + [vmem] * 3,
        out_specs=[smem] + [vmem] * 5,
        out_shape=[
            jax.ShapeDtypeStruct((SIZE,), I32),
            jax.ShapeDtypeStruct((3, MOST, 5 * width), BF),
            mask,
            mask,
            mask,
            jax.ShapeDtypeStruct((1, slab_rows), I32),
        ],
        scratch_shapes=[SMEM((NBLK + nocc,), I32), SMEM((4 * devices,), I32)],
        name="setup",
    )(place, occ, vir, occ_here, occ_lane, occ_rows)


def cost(micros):
    return pl.CostEstimate(flops=0, bytes_accessed=int(micros * 3_690_000), transcendentals=0)


def take_kernel(chips, table, *refs):
    for d in range(chips):
        refs[chips][d] = refs[d][...]


def take_for_sibling(table, amplitudes, first, count, cols_device):
    rows, width = amplitudes.shape[0], count * NBLK * BLK
    chips = amplitudes.shape[1] // cols_device // CORES
    step = 4 * NBLK * BLK
    per_device = cols_device // step

    def column(d):
        return lambda q, s: (0, (d * CORES + 1 - s[CORE]) * per_device + first // 4 + q)

    return pl.pallas_call(
        lambda *refs: take_kernel(chips, *refs),
        grid_spec=pltpu.PrefetchScalarGridSpec(
            num_scalar_prefetch=1,
            grid=(width // step,),
            in_specs=[pl.BlockSpec((rows, step), column(d)) for d in range(chips)],
            out_specs=pl.BlockSpec((chips, rows, step), lambda q, s: (0, 0, q)),
        ),
        out_shape=jax.ShapeDtypeStruct((chips, rows, width), amplitudes.dtype),
        cost_estimate=cost(1.5 + 0.5 * count),
        name="take_for_sibling",
    )(table, *[amplitudes] * chips)


def pack_kernel(count, table, own_ref, sib_ref, pick_ref, out_ref):
    pick = pick_ref[0]
    mine, other = half_masks(table, (own_ref.shape[0], LANE))

    def pair(u, carry):
        columns = []
        for c in (2 * u, 2 * u + 1):
            parts = [[], [], [], [], []]
            for ref, lead in ((own_ref, ()), (sib_ref, (0,))):
                at = lambda n: tile(ref, lead, c, table[n])
                parts[0].append(at(PURE))
                parts[1].append(at(PURE + 1))
                parts[2].append(at(TILE_W) * other + maybe_roll(at(TILE_B), table[ROLL]) * mine)
                parts[3].append(at(TILE_A) * mine)
                parts[4].append(maybe_roll(at(TILE_U), table[ROLL]) * other)
            columns.append(jnp.concatenate([x for part in parts for x in part], axis=0))
        rows = jnp.concatenate(columns, axis=1)
        lanes = pl.ds(pl.multiple_of(u * 2 * LANE, 2 * LANE), 2 * LANE)
        out_ref[0, :, lanes] = jnp.dot(pick, rows, preferred_element_type=F32).astype(BF)
        return carry

    lax.fori_loop(0, count // 2, pair, 0, unroll=2)


def pack(table, amplitudes, sibling, pick, cap, first, count, cols_device):
    rows, width = amplitudes.shape[0], count * NBLK * BLK
    chips = amplitudes.shape[1] // cols_device // CORES
    per_device = cols_device // width

    def column(d, s):
        return (0, (d * CORES + s[CORE]) * per_device + first // count)

    out = jax.ShapeDtypeStruct((chips, cap, count * LANE), BF)
    return pl.pallas_call(
        lambda *refs: pack_kernel(count, *refs),
        grid_spec=pltpu.PrefetchScalarGridSpec(
            num_scalar_prefetch=1,
            grid=(chips,),
            in_specs=[
                pl.BlockSpec((rows, width), column),
                pl.BlockSpec((1, rows, width), lambda d, s: (d, 0, 0)),
                pl.BlockSpec((1, cap, pick.shape[2]), lambda d, s: (s[KIND + d], 0, 0)),
            ],
            out_specs=pl.BlockSpec((1, cap, count * LANE), lambda d, s: (d, 0, 0)),
        ),
        out_shape=out,
        compiler_params=pltpu.CompilerParams(vmem_limit_bytes=GRANT),
        cost_estimate=cost(4 + 0.65 * count),
        name="pack",
    )(table, amplitudes, sibling, pick)


def spread_kernel(chips, cap, table, spread_ref):
    column = lax.broadcasted_iota(I32, (1, chips * cap), 1)
    row = lax.broadcasted_iota(I32, (ROWCAP, chips * cap), 0)
    for section, (n, f) in enumerate(((0, 0), (0, 1), (0, 2), (1, 3), (2, 3))):
        target = jnp.full((1, chips * cap), -1, I32)
        for d in range(chips):
            chip = d
            group = table[ROLE + n]
            k = column - d * cap - f * table[COUNT + table[ROLE] * chips + chip]
            count = table[COUNT + group * chips + chip]
            start = table[START + (group * chips + chip) * CORES]
            inside = (column >= d * cap) & (column < (d + 1) * cap) & (k >= 0) & (k < count)
            target = jnp.where(inside, start + k, target)
        spread_ref[section * ROWCAP : (section + 1) * ROWCAP, :] = jnp.where(row == target, 1.0, 0.0).astype(BF)


def make_spread(table, chips, cap):
    return pl.pallas_call(
        lambda *refs: spread_kernel(chips, cap, *refs),
        in_specs=[pl.BlockSpec(memory_space=SMEM)],
        out_specs=pl.BlockSpec(memory_space=VMEM),
        out_shape=jax.ShapeDtypeStruct((5 * ROWCAP, chips * cap), BF),
        compiler_params=pltpu.CompilerParams(vmem_limit_bytes=GRANT),
        cost_estimate=cost(1),
        name="make_spread",
    )(table)


def contract_kernel(table, got_ref, vals, spread_ref, big_ref, a_ref, b_ref, acc_ref, out_ref):

    @pl.when(pl.program_id(0) == 0)
    def _():
        out_ref[...] = acc_ref[...]

    received = got_ref[...].reshape(-1, got_ref.shape[2])
    spread = jnp.dot(spread_ref[...], received, preferred_element_type=F32)
    left = [spread[j * ROWCAP : (j + 1) * ROWCAP] for j in range(5)]
    half = (lax.broadcasted_iota(I32, (ROWCAP, 2 * LANE), 1) % LANE) // BLK
    left = [x.astype(BF) for x in left[:3] + [jnp.where(half == table[HALF], left[3], left[4])]]
    mine, other = half_masks(table, (vals.shape[0], LANE))
    right = [[], [], [], []]
    for c in (0, 1):
        at = lambda n: tile(vals, (), c, table[n])
        right[0].append(at(PURE) * big_ref[...])
        right[1].append(at(PURE + 1) * big_ref[...])
        right[2].append((at(TILE_W) * other + maybe_roll(at(TILE_B), table[ROLL]) * mine) * big_ref[...])
        right[3].append(at(TILE_A) * a_ref[...] + maybe_roll(at(TILE_U), table[ROLL]) * b_ref[...])
    right = jnp.concatenate([x for part in right for x in part], axis=1)
    out_ref[...] += contract(right, jnp.concatenate(left, axis=1))


def contract_chunk(table, received, integrals, spread, masks, acc, first, count):
    chips, cap = received.shape[:2]
    slab = integrals.shape[0]
    fixed = lambda u, s: (0, 0)
    return pl.pallas_call(
        contract_kernel,
        grid_spec=pltpu.PrefetchScalarGridSpec(
            num_scalar_prefetch=1,
            grid=(count // 2,),
            in_specs=[pl.BlockSpec((chips, cap, 2 * LANE), lambda u, s: (0, 0, u))]
            + [pl.BlockSpec((slab, 2 * NBLK * BLK), lambda u, s: (0, first // 2 + u))]
            + [pl.BlockSpec(x.shape, fixed) for x in (spread, *masks, acc)],
            out_specs=pl.BlockSpec(acc.shape, fixed),
        ),
        out_shape=jax.ShapeDtypeStruct(acc.shape, F32),
        compiler_params=pltpu.CompilerParams(vmem_limit_bytes=GRANT),
        cost_estimate=cost(1.5 + 1.3 * count),
        name="contract_chunk",
    )(table, received, integrals, spread, *masks, acc)


def split_kernel(chips, cap, table, sums_ref, class_ref, own_ref, sib_ref, held):
    d = pl.program_id(0)

    @pl.when(d == 0)
    def _():
        held[:ROWCAP, :] = sums_ref[...].T
        held[ROWCAP:, :] = jnp.zeros((cap + SUB, held.shape[1]), F32)

    kind = class_ref[...]
    for flip, ref in ((0, own_ref), (1, sib_ref)):
        device = d * CORES + (table[CORE] ^ flip)
        rows = []
        for n in range(3):
            start = table[START + table[SLAB + n] * chips * CORES + device]
            odd = start % SUB
            window = held[pl.ds(pl.multiple_of(start - odd, SUB), cap + SUB), :]
            rows.append(pltpu.roll(window, (cap + SUB - odd) % (cap + SUB), 0)[:cap])
        ref[0] = jnp.where(kind == table[SLAB], rows[0], jnp.where(kind == table[SLAB + 1], rows[1], rows[2]))


def split(table, sums, column_class, chips, cap):
    slab = sums.shape[0]
    out = jax.ShapeDtypeStruct((chips, cap, slab), F32)
    fixed = lambda d, s: (0, 0)
    return pl.pallas_call(
        lambda *refs: split_kernel(chips, cap, *refs),
        grid_spec=pltpu.PrefetchScalarGridSpec(
            num_scalar_prefetch=1,
            grid=(chips,),
            in_specs=[pl.BlockSpec(sums.shape, fixed), pl.BlockSpec((1, slab), fixed)],
            out_specs=[pl.BlockSpec((1, cap, slab), lambda d, s: (d, 0, 0))] * 2,
            scratch_shapes=[pltpu.VMEM((ROWCAP + cap + SUB, slab), F32)],
        ),
        out_shape=[out, out],
        cost_estimate=cost(6),
        name="split_sums",
    )(table, sums, column_class)


def finish_kernel(pairs, table, energies, class_ref, slab_ref, parts, out_ref, held):
    total = parts[0]
    for n in range(1, parts.shape[0]):
        total = total + parts[n]
    held[...] = total

    def one(p, carry):
        kind = table[ROW_CLASS + p]
        row = held[pl.ds(jnp.where(kind < 4, table[ROW_RANK + p], 0), 1), :]
        kept = jnp.where(class_ref[...] == kind, row, 0.0)
        out_ref[pl.ds(p, 1), :] = kept / (slab_ref[...] - energies[p])
        return carry

    lax.fori_loop(0, pairs, one, 0)


def finish(table, parts, energies, column_class, slab_energy):
    pairs, slab = energies.shape[0], column_class.shape[1]
    smem, vmem = pl.BlockSpec(memory_space=SMEM), pl.BlockSpec(memory_space=VMEM)
    return pl.pallas_call(
        lambda *refs: finish_kernel(pairs, *refs),
        in_specs=[smem] * 2 + [vmem] * 3,
        out_specs=vmem,
        out_shape=jax.ShapeDtypeStruct((pairs, slab), F32),
        scratch_shapes=[pltpu.VMEM(parts.shape[1:], F32)],
        cost_estimate=pl.CostEstimate(flops=4 * pairs * slab, bytes_accessed=8 * pairs * slab, transcendentals=0),
        name="finish",
    )(table, energies, column_class, slab_energy, parts)


def body(amplitudes, integrals, occ_irrep, vir_irrep, occ_energy, vir_energy):
    devices = lax.axis_size("wide")
    pairs_local = amplitudes.shape[0]
    cols = integrals.shape[1]
    slab_rows = integrals.shape[0]
    nvir = vir_energy.shape[0]
    nocc = occ_irrep.shape[0]
    given = (amplitudes, integrals, occ_irrep, vir_irrep, occ_energy, vir_energy)
    compact = (
        nvir == NBLK * BLK
        and CORES * cols == BLK * nvir
        and cols == sum(count for _, count in CHUNKS) * nvir
        and pairs_local % 16 == 0
        and devices == 16
        and nocc == 32
        and devices * pairs_local == nocc * nocc
        and lax.axis_size("parts") == 2
    )
    if not compact:
        return dense_body(*given)

    chips = devices // CORES
    position = lax.axis_index("wide")
    place = jnp.stack([position // CORES, position % CORES]).astype(I32)
    swap = [(i, i ^ 1) for i in range(devices)]
    cores = [list(range(core, devices, CORES)) for core in range(CORES)]

    def exchange(x):
        return lax.all_to_all(x, "wide", 0, 0, axis_index_groups=cores, tiled=True)

    table, pick, big, mask_a, mask_b, column_class = setup(place, occ_irrep, vir_irrep, slab_rows, devices)
    level = table[LEVEL : LEVEL + 1]
    level = jnp.maximum(level, lax.ppermute(level, "parts", [(0, 1), (1, 0)]))[0]

    def take(n, after=None):
        at = place if after is None else lax.optimization_barrier((place, after))[0]
        return take_for_sibling(at, amplitudes, *CHUNKS[n], cols)

    first_take = take(0)
    early = (lax.ppermute(first_take, "wide", swap), take(1, first_take))

    def compact_plan(cap, cap_back):
        def run(amplitudes, integrals, early):
            spread = make_spread(table, chips, cap)
            sent = []
            siblings = [early[0], lax.ppermute(early[1], "wide", swap)]
            acc = jnp.zeros((slab_rows, ROWCAP), F32)
            received = []
            for n, (first, count) in enumerate(CHUNKS):
                packed = pack(table, amplitudes, siblings[n], pick, cap, first, count, cols)
                if n + 2 < len(CHUNKS):
                    siblings.append(lax.ppermute(take(n + 2, packed), "wide", swap))
                received.append(exchange(packed))
            for n, (first, count) in enumerate(CHUNKS):
                acc = contract_chunk(table, received[n], integrals, spread, (big, mask_a, mask_b), acc, first, count)
            own, other = split(table, acc, column_class, chips, cap_back)
            back = exchange(own + lax.ppermute(other, "wide", swap))
            slab_energy = (vir_energy[: slab_rows // nvir, None] + vir_energy[None, :]).reshape(1, -1)
            pair_energy = (occ_energy[:, None] + occ_energy[None, :]).reshape(-1)
            own_energy = lax.dynamic_slice_in_dim(pair_energy, position * pairs_local, pairs_local, 0)
            return finish(table, back, own_energy, column_class, slab_energy)

        return run

    def dense_plan(amplitudes, integrals, early):
        return dense_body(amplitudes, integrals, *given[2:])

    plans = [compact_plan(n, m) for n, m in LEVELS] + [dense_plan]
    usual = lambda *held: lax.switch(level, plans[:2], *held)
    rare = lambda *held: lax.switch(level - 2, plans[2:], *held)
    return lax.cond(level < 2, usual, rare, amplitudes, integrals, early)


def solution(mesh):
    return jax.shard_map(
        body,
        mesh=mesh,
        in_specs=(
            P(("parts", "wide"), None),
            P("parts", "wide"),
            P("parts"),
            P("parts"),
            P("parts"),
            P("parts"),
        ),
        out_specs=P(("parts", "wide"), None),
        check_vma=False,
    )
```

```python
import jax
import jax.numpy as jnp
from jax import lax
from jax.experimental import pallas as pl
from jax.experimental.pallas import tpu as pltpu
from jax.sharding import PartitionSpec as P

BLK = 64
LANE = 128
SUB = 8
NBLK = 8
CORES = 2
ROWCAP = 256
CHUNKS = ((0, 8), (16, 16), (8, 8))
LEVELS = ((96, 24), (112, 24), (144, 24))
MOST = max(cap for cap, _ in LEVELS)
CHIP, CORE, PURE, TILE_A, TILE_B, ROLL, TILE_U, TILE_W, HALF, KIND, ROLE, LEVEL, SLAB = 0, 1, 2, 4, 5, 6, 7, 8, 9, 16, 24, 27, 28
START, COUNT, ROW_CLASS, ROW_RANK, SIZE = 32, 96, 128, 192, 256
TYPES = ((0, 1, 2), (1, 0, 3), (2, 3, 0))
SMEM = pltpu.SMEM
VMEM = pltpu.VMEM
GRANT = 48 * 1024 * 1024
BF = jnp.bfloat16
F32 = jnp.float32
I32 = jnp.int32


def block_lookup(table, block_ids):
    labels = jnp.arange(table.shape[0], dtype=jnp.int32)
    hits = block_ids[:, None] == labels[None, :]
    return jnp.sum(jnp.where(hits, table[None, :], 0), axis=1)


def contract(left, right):
    return lax.dot_general(
        left, right, (((1,), (1,)), ((), ())), preferred_element_type=jnp.float32
    )


def dense_body(amplitudes, integrals, occ_irrep, vir_irrep, occ_energy, vir_energy):
    position = lax.axis_index("wide")
    pairs_local = amplitudes.shape[0]
    local_cols = integrals.shape[1]
    nvir = vir_energy.shape[0]
    slab_rows = integrals.shape[0]
    slab_first = slab_rows // nvir
    gathered = lax.all_to_all(amplitudes, "wide", split_axis=1, concat_axis=0, tiled=True)
    flat_cols = position * local_cols + jnp.arange(local_cols, dtype=jnp.int32)
    first_vir = flat_cols // nvir
    second_vir = flat_cols % nvir
    col_irrep = jnp.bitwise_xor(
        block_lookup(vir_irrep, first_vir // BLK), block_lookup(vir_irrep, second_vir // BLK)
    )
    vir_label = block_lookup(vir_irrep, jnp.arange(nvir, dtype=jnp.int32) // BLK)
    pair_irrep = jnp.bitwise_xor(occ_irrep[:, None], occ_irrep[None, :]).reshape(-1)
    slab_irrep = jnp.bitwise_xor(vir_label[:slab_first, None], vir_label[None, :]).reshape(-1)
    kept_t = jnp.where(pair_irrep[:, None] == col_irrep[None, :], gathered, 0)
    kept_v = jnp.where(slab_irrep[:, None] == col_irrep[None, :], integrals, 0)
    summed = lax.psum_scatter(contract(kept_t, kept_v), "wide", scatter_dimension=0, tiled=True)
    slab_energy = (vir_energy[:slab_first, None] + vir_energy[None, :]).reshape(-1)
    pair_energy = (occ_energy[:, None] + occ_energy[None, :]).reshape(-1)
    local_pair_energy = lax.dynamic_slice_in_dim(
        pair_energy, position * pairs_local, pairs_local, 0
    )
    denominator = slab_energy[None, :] - local_pair_energy[:, None]
    return summed / denominator


def tile(ref, lead, c, which):
    start = pl.multiple_of(c * NBLK * BLK + which * LANE, LANE)
    return ref[lead + (slice(None), pl.ds(start, LANE))]


def maybe_roll(x, flag):
    return jnp.where(flag == 1, jnp.concatenate([x[:, BLK:], x[:, :BLK]], axis=1), x)


def half_masks(table, shape):
    half = (lax.broadcasted_iota(I32, shape, 1) % LANE) // BLK
    first = half == table[HALF]
    return jnp.where(first, 1.0, 0.0).astype(BF), jnp.where(first, 0.0, 1.0).astype(BF)


def setup_kernel(
    devices, nslab, place, occ, vir, occ_here, occ_lane, occ_rows, table, pick_ref, big_ref, a_ref, b_ref, class_ref, hist, tally
):
    chips = devices // CORES
    nocc = occ.shape[0]
    per_device = nocc // devices
    chip, core = place[0], place[1]
    table[CHIP] = chip
    table[CORE] = core
    common, zero_at, seven_at = vir[0] * 0, vir[0] * 0, vir[0] * 0
    for b in range(NBLK):
        label = vir[b]
        common = jnp.where((label != 0) & (label != 7), label, common)
        zero_at = jnp.where(label == 0, b, zero_at)
        seven_at = jnp.where(label == 7, b, seven_at)
        table[KIND + b] = jnp.where(label == 0, 1, jnp.where(label == 7, 2, 0))
    irreps = [common * 0, common, common ^ 7, common * 0 + 7]
    needed = []
    for g in range(4):
        some = common * 0
        for b in range(NBLK):
            some = jnp.where((vir[0] ^ vir[b]) == irreps[g], 1, some)
        needed.append(some)

    tile_a, half_a = zero_at // 2, zero_at % 2
    same = seven_at // 2 == tile_a
    tile_b = jnp.where(same, (tile_a + 1) % 4, seven_at // 2)
    pure = jnp.where((tile_a != 0) & (tile_b != 0), 0, jnp.where((tile_a != 1) & (tile_b != 1), 1, 2))
    table[PURE] = pure
    table[PURE + 1] = 6 - tile_a - tile_b - pure
    table[TILE_A] = tile_a
    table[TILE_B] = tile_b
    table[ROLL] = jnp.where(same | (seven_at % 2 != half_a), 0, 1)
    table[TILE_U] = jnp.where(same, tile_a, tile_b)
    table[TILE_W] = jnp.where(same, tile_b, tile_a)
    table[HALF] = half_a

    for h in range(NBLK):
        hist[h] = 0
    for j in range(nocc):
        hist[NBLK + j] = hist[occ[j]]
        hist[occ[j]] = hist[occ[j]] + 1
    of_i = lambda i, g: hist[occ[i] ^ irreps[g]] * needed[g]
    biggest = common * 0
    most_class = common * 0
    for g in range(4):
        total = common * 0
        for s in range(devices):
            table[START + g * devices + s] = total
            here = common * 0
            for i in range(per_device):
                here += of_i(s * per_device + i, g)
            total += here
            biggest = jnp.maximum(biggest, here)
            tally[g * devices + s] = here
        most_class = jnp.maximum(most_class, total)
        for c in range(chips):
            table[COUNT + g * chips + c] = tally[g * devices + c * CORES] + tally[g * devices + c * CORES + 1]
    most = common * 0
    for c in range(chips):
        n = [table[COUNT + g * chips + c] for g in range(4)]
        for b, a, s in TYPES:
            most = jnp.maximum(most, 3 * n[b] + jnp.maximum(n[a], n[s]))
    level = common * 0 + len(LEVELS)
    for at in range(len(LEVELS) - 1, -1, -1):
        cap, cap_back = LEVELS[at]
        level = jnp.where((most <= cap) & (biggest <= cap_back) & (most_class <= ROWCAP), at, level)
    table[LEVEL] = level

    roles_of = lambda kind: [jnp.where(kind == 0, x, jnp.where(kind == 1, y, z)) for x, y, z in zip(*TYPES)]
    roles, of_slab = roles_of(table[KIND + chip]), roles_of(table[KIND])
    for n in range(3):
        table[ROLE + n] = roles[n]
        table[SLAB + n] = of_slab[n]
    position = chip * CORES + core
    for i in range(per_device):
        at = position * per_device + i
        for j in range(nocc):
            both = occ[at] ^ occ[j]
            kind = common * 0 + 4
            rank = hist[NBLK + j]
            for g in range(4):
                hit = (both == irreps[g]) & (needed[g] == 1)
                kind = jnp.where(hit, g, kind)
                for before in range(i):
                    rank = rank + jnp.where(hit, of_i(position * per_device + before, g), 0)
            table[ROW_CLASS + i * nocc + j] = kind
            table[ROW_RANK + i * nocc + j] = rank

    width = CORES * per_device * nocc
    lane = lax.broadcasted_iota(I32, (1, width), 1)
    earlier = lax.broadcasted_iota(I32, (nocc, width), 0) < lax.broadcasted_iota(I32, (nocc, width), 1) % nocc
    alike = jnp.where((occ_rows[...] == occ_lane[...]) & earlier, 1, 0)
    rank = jnp.sum(alike, axis=0, keepdims=True)
    irrep = occ_lane[...] ^ occ_here[...]
    spots = []
    for g in range(4):
        base, run = jnp.zeros((1, width), I32), common * 0
        for i in range(CORES * per_device):
            shown = i ^ (core * per_device)
            base = jnp.where(lane // nocc == shown, run, base)
            run += of_i(chip * CORES * per_device + i, g)
        spots.append((jnp.where((irrep == irreps[g]) & (needed[g] == 1), base + rank, -4 * MOST), run))
    slot = lax.broadcasted_iota(I32, (MOST, width), 0)
    for t, (b, a, s) in enumerate(TYPES):
        for section, (g, f) in enumerate(((b, 0), (b, 1), (b, 2), (a, 3), (s, 3))):
            target = spots[g][0] + f * spots[b][1]
            pick_ref[t, :, section * width : (section + 1) * width] = jnp.where(slot == target, 1.0, 0.0).astype(BF)

    half = lax.broadcasted_iota(I32, (BLK, LANE), 1) // BLK == half_a
    column = lax.broadcasted_iota(I32, class_ref.shape, 1) % (NBLK * BLK) // BLK
    column_class = jnp.zeros(class_ref.shape, I32)
    for b in range(NBLK):
        both = vir[0] ^ vir[b]
        kind = common * 0 + 4
        for g in range(4):
            kind = jnp.where(both == irreps[g], g, kind)
        column_class = jnp.where(column == b, kind, column_class)
        is_ = [jnp.where(kind == roles[n], 1.0, 0.0) for n in range(3)]
        full = jnp.zeros((BLK, LANE), F32)
        for a in range(nslab):
            rows = slice((a * NBLK + b) * BLK, (a * NBLK + b + 1) * BLK)
            big_ref[rows, :] = (full + is_[0]).astype(BF)
            a_ref[rows, :] = jnp.where(half, full + is_[1], 0.0).astype(BF)
            b_ref[rows, :] = jnp.where(half, 0.0, full + is_[2]).astype(BF)
    class_ref[...] = column_class


def setup(place, occ, vir, slab_rows, devices):
    nocc = occ.shape[0]
    width = CORES * nocc // devices * nocc
    per_chip = width // nocc
    chip, core = place[0], place[1]
    mine = lax.dynamic_slice_in_dim(occ, chip * per_chip, per_chip, 0).reshape(CORES, -1)
    mine = jnp.where(core == 0, mine, mine[::-1]).reshape(-1)
    occ_here = jnp.repeat(mine, nocc)[None, :]
    occ_lane = jnp.tile(occ, per_chip)[None, :]
    occ_rows = jnp.broadcast_to(occ[:, None], (nocc, width))
    smem, vmem = pl.BlockSpec(memory_space=SMEM), pl.BlockSpec(memory_space=VMEM)
    mask = jax.ShapeDtypeStruct((slab_rows, LANE), BF)
    return pl.pallas_call(
        lambda *refs: setup_kernel(devices, slab_rows // (NBLK * BLK), *refs),
        in_specs=[smem] * 3 + [vmem] * 3,
        out_specs=[smem] + [vmem] * 5,
        out_shape=[
            jax.ShapeDtypeStruct((SIZE,), I32),
            jax.ShapeDtypeStruct((3, MOST, 5 * width), BF),
            mask,
            mask,
            mask,
            jax.ShapeDtypeStruct((1, slab_rows), I32),
        ],
        scratch_shapes=[SMEM((NBLK + nocc,), I32), SMEM((4 * devices,), I32)],
        name="setup",
    )(place, occ, vir, occ_here, occ_lane, occ_rows)


def cost(micros):
    return pl.CostEstimate(flops=0, bytes_accessed=int(micros * 3_690_000), transcendentals=0)


def take_kernel(chips, table, *refs):
    for d in range(chips):
        refs[chips][d] = refs[d][...]


def take_for_sibling(table, amplitudes, first, count, cols_device):
    rows, width = amplitudes.shape[0], count * NBLK * BLK
    chips = amplitudes.shape[1] // cols_device // CORES
    step = 4 * NBLK * BLK
    per_device = cols_device // step

    def column(d):
        return lambda q, s: (0, (d * CORES + 1 - s[CORE]) * per_device + first // 4 + q)

    return pl.pallas_call(
        lambda *refs: take_kernel(chips, *refs),
        grid_spec=pltpu.PrefetchScalarGridSpec(
            num_scalar_prefetch=1,
            grid=(width // step,),
            in_specs=[pl.BlockSpec((rows, step), column(d)) for d in range(chips)],
            out_specs=pl.BlockSpec((chips, rows, step), lambda q, s: (0, 0, q)),
        ),
        out_shape=jax.ShapeDtypeStruct((chips, rows, width), amplitudes.dtype),
        cost_estimate=cost(1.5 + 0.5 * count),
        name="take_for_sibling",
    )(table, *[amplitudes] * chips)


def pack_kernel(count, table, own_ref, sib_ref, pick_ref, out_ref):
    pick = pick_ref[0]
    mine, other = half_masks(table, (own_ref.shape[0], LANE))

    def pair(u, carry):
        columns = []
        for c in (2 * u, 2 * u + 1):
            parts = [[], [], [], [], []]
            for ref, lead in ((own_ref, ()), (sib_ref, (0,))):
                at = lambda n: tile(ref, lead, c, table[n])
                parts[0].append(at(PURE))
                parts[1].append(at(PURE + 1))
                parts[2].append(at(TILE_W) * other + maybe_roll(at(TILE_B), table[ROLL]) * mine)
                parts[3].append(at(TILE_A) * mine)
                parts[4].append(maybe_roll(at(TILE_U), table[ROLL]) * other)
            columns.append(jnp.concatenate([x for part in parts for x in part], axis=0))
        rows = jnp.concatenate(columns, axis=1)
        lanes = pl.ds(pl.multiple_of(u * 2 * LANE, 2 * LANE), 2 * LANE)
        out_ref[0, :, lanes] = jnp.dot(pick, rows, preferred_element_type=F32).astype(BF)
        return carry

    lax.fori_loop(0, count // 2, pair, 0, unroll=4)


def pack(table, amplitudes, sibling, pick, cap, first, count, cols_device):
    rows, width = amplitudes.shape[0], count * NBLK * BLK
    chips = amplitudes.shape[1] // cols_device // CORES
    per_device = cols_device // width

    def column(d, s):
        return (0, (d * CORES + s[CORE]) * per_device + first // count)

    out = jax.ShapeDtypeStruct((chips, cap, count * LANE), BF)
    return pl.pallas_call(
        lambda *refs: pack_kernel(count, *refs),
        grid_spec=pltpu.PrefetchScalarGridSpec(
            num_scalar_prefetch=1,
            grid=(chips,),
            in_specs=[
                pl.BlockSpec((rows, width), column),
                pl.BlockSpec((1, rows, width), lambda d, s: (d, 0, 0)),
                pl.BlockSpec((1, cap, pick.shape[2]), lambda d, s: (s[KIND + d], 0, 0)),
            ],
            out_specs=pl.BlockSpec((1, cap, count * LANE), lambda d, s: (d, 0, 0)),
        ),
        out_shape=out,
        compiler_params=pltpu.CompilerParams(vmem_limit_bytes=GRANT),
        cost_estimate=cost(4 + 0.65 * count),
        name="pack",
    )(table, amplitudes, sibling, pick)


def spread_kernel(chips, cap, table, spread_ref):
    column = lax.broadcasted_iota(I32, (1, chips * cap), 1)
    row = lax.broadcasted_iota(I32, (ROWCAP, chips * cap), 0)
    for section, (n, f) in enumerate(((0, 0), (0, 1), (0, 2), (1, 3), (2, 3))):
        target = jnp.full((1, chips * cap), -1, I32)
        for d in range(chips):
            chip = d
            group = table[ROLE + n]
            k = column - d * cap - f * table[COUNT + table[ROLE] * chips + chip]
            count = table[COUNT + group * chips + chip]
            start = table[START + (group * chips + chip) * CORES]
            inside = (column >= d * cap) & (column < (d + 1) * cap) & (k >= 0) & (k < count)
            target = jnp.where(inside, start + k, target)
        spread_ref[section * ROWCAP : (section + 1) * ROWCAP, :] = jnp.where(row == target, 1.0, 0.0).astype(BF)


def make_spread(table, chips, cap):
    return pl.pallas_call(
        lambda *refs: spread_kernel(chips, cap, *refs),
        in_specs=[pl.BlockSpec(memory_space=SMEM)],
        out_specs=pl.BlockSpec(memory_space=VMEM),
        out_shape=jax.ShapeDtypeStruct((5 * ROWCAP, chips * cap), BF),
        compiler_params=pltpu.CompilerParams(vmem_limit_bytes=GRANT),
        cost_estimate=cost(1),
        name="make_spread",
    )(table)


def contract_kernel(table, got_ref, vals, spread_ref, big_ref, a_ref, b_ref, acc_ref, out_ref):

    @pl.when(pl.program_id(0) == 0)
    def _():
        out_ref[...] = acc_ref[...]

    received = got_ref[...].reshape(-1, got_ref.shape[2])
    spread = jnp.dot(spread_ref[...], received, preferred_element_type=F32)
    left = [spread[j * ROWCAP : (j + 1) * ROWCAP] for j in range(5)]
    half = (lax.broadcasted_iota(I32, (ROWCAP, 2 * LANE), 1) % LANE) // BLK
    left = [x.astype(BF) for x in left[:3] + [jnp.where(half == table[HALF], left[3], left[4])]]
    mine, other = half_masks(table, (vals.shape[0], LANE))
    right = [[], [], [], []]
    for c in (0, 1):
        at = lambda n: tile(vals, (), c, table[n])
        right[0].append(at(PURE) * big_ref[...])
        right[1].append(at(PURE + 1) * big_ref[...])
        right[2].append((at(TILE_W) * other + maybe_roll(at(TILE_B), table[ROLL]) * mine) * big_ref[...])
        right[3].append(at(TILE_A) * a_ref[...] + maybe_roll(at(TILE_U), table[ROLL]) * b_ref[...])
    right = jnp.concatenate([x for part in right for x in part], axis=1)
    out_ref[...] += contract(right, jnp.concatenate(left, axis=1))


def contract_chunk(table, received, integrals, spread, masks, acc, first, count):
    chips, cap = received.shape[:2]
    slab = integrals.shape[0]
    fixed = lambda u, s: (0, 0)
    return pl.pallas_call(
        contract_kernel,
        grid_spec=pltpu.PrefetchScalarGridSpec(
            num_scalar_prefetch=1,
            grid=(count // 2,),
            in_specs=[pl.BlockSpec((chips, cap, 2 * LANE), lambda u, s: (0, 0, u))]
            + [pl.BlockSpec((slab, 2 * NBLK * BLK), lambda u, s: (0, first // 2 + u))]
            + [pl.BlockSpec(x.shape, fixed) for x in (spread, *masks, acc)],
            out_specs=pl.BlockSpec(acc.shape, fixed),
        ),
        out_shape=jax.ShapeDtypeStruct(acc.shape, F32),
        compiler_params=pltpu.CompilerParams(vmem_limit_bytes=GRANT),
        cost_estimate=cost(1.5 + 1.3 * count),
        name="contract_chunk",
    )(table, received, integrals, spread, *masks, acc)


def split_kernel(chips, cap, table, sums_ref, class_ref, own_ref, sib_ref, held):
    d = pl.program_id(0)

    @pl.when(d == 0)
    def _():
        held[:ROWCAP, :] = sums_ref[...].T
        held[ROWCAP:, :] = jnp.zeros((cap + SUB, held.shape[1]), F32)

    kind = class_ref[...]
    for flip, ref in ((0, own_ref), (1, sib_ref)):
        device = d * CORES + (table[CORE] ^ flip)
        rows = []
        for n in range(3):
            start = table[START + table[SLAB + n] * chips * CORES + device]
            odd = start % SUB
            window = held[pl.ds(pl.multiple_of(start - odd, SUB), cap + SUB), :]
            rows.append(pltpu.roll(window, (cap + SUB - odd) % (cap + SUB), 0)[:cap])
        ref[0] = jnp.where(kind == table[SLAB], rows[0], jnp.where(kind == table[SLAB + 1], rows[1], rows[2]))


def split(table, sums, column_class, chips, cap):
    slab = sums.shape[0]
    out = jax.ShapeDtypeStruct((chips, cap, slab), F32)
    fixed = lambda d, s: (0, 0)
    return pl.pallas_call(
        lambda *refs: split_kernel(chips, cap, *refs),
        grid_spec=pltpu.PrefetchScalarGridSpec(
            num_scalar_prefetch=1,
            grid=(chips,),
            in_specs=[pl.BlockSpec(sums.shape, fixed), pl.BlockSpec((1, slab), fixed)],
            out_specs=[pl.BlockSpec((1, cap, slab), lambda d, s: (d, 0, 0))] * 2,
            scratch_shapes=[pltpu.VMEM((ROWCAP + cap + SUB, slab), F32)],
        ),
        out_shape=[out, out],
        cost_estimate=cost(6),
        name="split_sums",
    )(table, sums, column_class)


def finish_kernel(pairs, table, energies, class_ref, slab_ref, parts, out_ref, held):
    total = parts[0]
    for n in range(1, parts.shape[0]):
        total = total + parts[n]
    held[...] = total

    def one(p, carry):
        kind = table[ROW_CLASS + p]
        row = held[pl.ds(jnp.where(kind < 4, table[ROW_RANK + p], 0), 1), :]
        kept = jnp.where(class_ref[...] == kind, row, 0.0)
        out_ref[pl.ds(p, 1), :] = kept / (slab_ref[...] - energies[p])
        return carry

    lax.fori_loop(0, pairs, one, 0, unroll=8)


def finish(table, parts, energies, column_class, slab_energy):
    pairs, slab = energies.shape[0], column_class.shape[1]
    smem, vmem = pl.BlockSpec(memory_space=SMEM), pl.BlockSpec(memory_space=VMEM)
    return pl.pallas_call(
        lambda *refs: finish_kernel(pairs, *refs),
        in_specs=[smem] * 2 + [vmem] * 3,
        out_specs=vmem,
        out_shape=jax.ShapeDtypeStruct((pairs, slab), F32),
        scratch_shapes=[pltpu.VMEM(parts.shape[1:], F32)],
        cost_estimate=pl.CostEstimate(flops=4 * pairs * slab, bytes_accessed=8 * pairs * slab, transcendentals=0),
        name="finish",
    )(table, energies, column_class, slab_energy, parts)


def body(amplitudes, integrals, occ_irrep, vir_irrep, occ_energy, vir_energy):
    devices = lax.axis_size("wide")
    pairs_local = amplitudes.shape[0]
    cols = integrals.shape[1]
    slab_rows = integrals.shape[0]
    nvir = vir_energy.shape[0]
    nocc = occ_irrep.shape[0]
    given = (amplitudes, integrals, occ_irrep, vir_irrep, occ_energy, vir_energy)
    compact = (
        nvir == NBLK * BLK
        and CORES * cols == BLK * nvir
        and cols == sum(count for _, count in CHUNKS) * nvir
        and pairs_local % 16 == 0
        and devices == 16
        and nocc == 32
        and devices * pairs_local == nocc * nocc
        and lax.axis_size("parts") == 2
    )
    if not compact:
        return dense_body(*given)

    chips = devices // CORES
    position = lax.axis_index("wide")
    place = jnp.stack([position // CORES, position % CORES]).astype(I32)
    swap = [(i, i ^ 1) for i in range(devices)]
    cores = [list(range(core, devices, CORES)) for core in range(CORES)]

    def exchange(x):
        return lax.all_to_all(x, "wide", 0, 0, axis_index_groups=cores, tiled=True)

    table, pick, big, mask_a, mask_b, column_class = setup(place, occ_irrep, vir_irrep, slab_rows, devices)
    level = table[LEVEL : LEVEL + 1]
    level = jnp.maximum(level, lax.ppermute(level, "parts", [(0, 1), (1, 0)]))[0]

    def take(n, after=None):
        at = place if after is None else lax.optimization_barrier((place, after))[0]
        return take_for_sibling(at, amplitudes, *CHUNKS[n], cols)

    first_take = take(0)
    early = (lax.ppermute(first_take, "wide", swap), take(1, first_take))

    def compact_plan(cap, cap_back):
        def run(amplitudes, integrals, early):
            spread = make_spread(table, chips, cap)
            sent = []
            siblings = [early[0], lax.ppermute(early[1], "wide", swap)]
            acc = jnp.zeros((slab_rows, ROWCAP), F32)
            received = []
            for n, (first, count) in enumerate(CHUNKS):
                packed = pack(table, amplitudes, siblings[n], pick, cap, first, count, cols)
                if n + 2 < len(CHUNKS):
                    siblings.append(lax.ppermute(take(n + 2, packed), "wide", swap))
                received.append(exchange(packed))
            for n, (first, count) in enumerate(CHUNKS):
                acc = contract_chunk(table, received[n], integrals, spread, (big, mask_a, mask_b), acc, first, count)
            own, other = split(table, acc, column_class, chips, cap_back)
            back = exchange(own + lax.ppermute(other, "wide", swap))
            slab_energy = (vir_energy[: slab_rows // nvir, None] + vir_energy[None, :]).reshape(1, -1)
            pair_energy = (occ_energy[:, None] + occ_energy[None, :]).reshape(-1)
            own_energy = lax.dynamic_slice_in_dim(pair_energy, position * pairs_local, pairs_local, 0)
            return finish(table, back, own_energy, column_class, slab_energy)

        return run

    def dense_plan(amplitudes, integrals, early):
        return dense_body(amplitudes, integrals, *given[2:])

    plans = [compact_plan(n, m) for n, m in LEVELS] + [dense_plan]
    usual = lambda *held: lax.switch(level, plans[:2], *held)
    rare = lambda *held: lax.switch(level - 2, plans[2:], *held)
    return lax.cond(level < 2, usual, rare, amplitudes, integrals, early)


def solution(mesh):
    return jax.shard_map(
        body,
        mesh=mesh,
        in_specs=(
            P(("parts", "wide"), None),
            P("parts", "wide"),
            P("parts"),
            P("parts"),
            P("parts"),
            P("parts"),
        ),
        out_specs=P(("parts", "wide"), None),
        check_vma=False,
    )
```
